32 devices in a mesh: dp: 16 (over z, x, core), tensor: 2 (over y).
Axes of the slice: x: 2, y: 2, z: 4, core: 2. Of those that a mesh axis runs over, the one named last changes fastest.
Arguments:
- tokens: bfloat16 [87680, 1024], P(('dp', 'tensor')), may hold values from -6 to 6
- cotangent: bfloat16 [87680, 1024], P(('dp', 'tensor')), may hold values from -12 to 12
- attention_gain: bfloat16 [1024], P('dp'), may hold values from 0.5 to 1.5
- attention_shift: bfloat16 [1024], P('dp'), may hold values from -1.75 to 1.75
- triple_weight: bfloat16 [1024, 3, 1024], P('dp', None, 'tensor'), may hold values from -0.25 to 0.25
- query_bias: bfloat16 [1024], P('dp'), may hold values from -3 to 3
- value_bias: bfloat16 [1024], P('dp'), may hold values from -3 to 3
- merge_weight: bfloat16 [1024, 1024], P('dp', 'tensor'), may hold values from -0.75 to 0.75
- merge_bias: bfloat16 [1024], P('dp'), may hold values from -1.75 to 1.75
- attention_scale: bfloat16 [1024], P('dp'), may hold values from 0.25 to 1.75
- forward_gain: bfloat16 [1024], P('dp'), may hold values from 0.5 to 1.5
- forward_shift: bfloat16 [1024], P('dp'), may hold values from -1.75 to 1.75
- expand_weight: bfloat16 [1024, 4096], P('dp', 'tensor'), may hold values from -0.1875 to 0.1875
- expand_bias: bfloat16 [4096], P('dp'), may hold values from -3 to 3
- reduce_weight: bfloat16 [1024, 4096], P('dp', 'tensor'), may hold values from -0.1875 to 0.1875
- reduce_bias: bfloat16 [1024], P('dp'), may hold values from -1.75 to 1.75
- forward_scale: bfloat16 [1024], P('dp'), may hold values from 0.25 to 1.75
Outputs:
- result: bfloat16 [87680, 1024], P(('dp', 'tensor'))
- tokens_gradient: bfloat16 [87680, 1024], P(('dp', 'tensor'))
- attention_gain_gradient: float32 [1024], P('dp')
- attention_shift_gradient: float32 [1024], P('dp')
- triple_weight_gradient: float32 [1024, 3, 1024], P('dp', None, 'tensor')
- query_bias_gradient: float32 [1024], P('dp')
- value_bias_gradient: float32 [1024], P('dp')
- merge_weight_gradient: float32 [1024, 1024], P('dp', 'tensor')
- merge_bias_gradient: float32 [1024], P('dp')
- attention_scale_gradient: float32 [1024], P('dp')
- forward_gain_gradient: float32 [1024], P('dp')
- forward_shift_gradient: float32 [1024], P('dp')
- expand_weight_gradient: float32 [1024, 4096], P('dp', 'tensor')
- expand_bias_gradient: float32 [4096], P('dp')
- reduce_weight_gradient: float32 [1024, 4096], P('dp', 'tensor')
- reduce_bias_gradient: float32 [1024], P('dp')
- forward_scale_gradient: float32 [1024], P('dp')
The draws below stay inside these ranges and needn't reach their ends.
All inputs are finite; a program needn't handle non-finite values.
Results may differ from the reference program's by a relative error of at most 0.022.
Values may be sent and summed in bfloat16 or wider, within the bound.
No kernel may reach another device: no remote copies, remote signals or barrier semaphores. Data moves between devices by JAX's collectives and lax.ppermute only.
A program may use at most 448 MiB of HBM per device.

```python
import jax
import jax.numpy as jnp
from jax import lax

D = 1024
H = 16
HD = 64
FF = 4096
SEQ = 1370
TOKENS = 87680


def raised(values, stream_key, source, target, parts, factor):
    owner, partner = [(jnp.arange(values.shape[dim]) // (values.shape[dim] // parts)).reshape([-1 if axis == dim else 1 for axis in range(values.ndim)]) for dim in (source, target)]
    chosen = jax.random.permutation(stream_key, parts)[partner]
    strong = (owner == chosen) | (owner == (partner + parts // 2) % parts)
    return jnp.where(strong, factor * values, values)


def block_scale(stream_key, extent, shards, least, top_value):
    level = 1.0
    for position, blocks in shards:
        steps = jax.random.uniform(jax.random.fold_in(jax.random.fold_in(stream_key, 6), position), (blocks,), jnp.float32, least / len(shards), top_value / len(shards))
        level = level * jnp.repeat(jnp.exp(steps), extent[position] // blocks).reshape((-1,) + (1,) * (len(extent) - 1 - position))
    return level


def noise(own_key, extent, deviation, most, split=(), kind=jnp.bfloat16):
    factor_of = block_scale(own_key, extent, split, -0.22, 0.18) if split else 1.0
    values = jax.random.normal(own_key, extent, jnp.float32) * deviation * factor_of
    return jnp.minimum(jnp.maximum(values, -most), most).astype(kind)


def bell_draw_with(stream_key, shape, deviation, bound, shards, heavy, dtype=jnp.bfloat16):
    entries = deviation * jax.random.normal(stream_key, shape, jnp.float32)
    if shards:
        entries = entries * block_scale(stream_key, shape, shards, -0.22, 0.18)
    return jnp.clip(raised(entries, jax.random.fold_in(stream_key, 3), *heavy), -bound, bound).astype(dtype)


def setup_inputs(seed: int = 0) -> dict:
    seeds = jax.random.split(jax.random.key(seed), 18)
    tokens = noise(seeds[0], (TOKENS, D), 1.0, 6.0, ((0, 32),))
    cotangent = bell_draw_with(seeds[1], (TOKENS, D), 1.0, 12.0, ((0, 32),), (0, 1, 32, 2.75))
    attention_gain = jnp.clip(1.0 + 0.1 * jax.random.normal(seeds[2], (D,), jnp.float32), 0.5, 1.5).astype(jnp.bfloat16)
    attention_shift = noise(seeds[3], (D,), 0.3, 1.75, ((0, 16),))
    triple_weight = noise(seeds[4], (D, 3, D), (D // 2) ** -0.5, 0.25, ((0, 16), (2, 2)))
    query_bias = noise(seeds[5], (D,), 0.5, 3.0, ((0, 16),))
    value_bias = noise(seeds[6], (D,), 0.5, 3.0, ((0, 16),))
    merge_weight = noise(seeds[7], (D, D), (D // 16) ** -0.5, 0.75, ((0, 16), (1, 2)))
    merge_bias = noise(seeds[8], (D,), 0.3, 1.75, ((0, 16),))
    attention_scale = jnp.clip(1.0 + 0.15 * jax.random.normal(seeds[9], (D,), jnp.float32), 0.25, 1.75).astype(jnp.bfloat16)
    forward_gain = jnp.clip(1.0 + 0.1 * jax.random.normal(seeds[10], (D,), jnp.float32), 0.5, 1.5).astype(jnp.bfloat16)
    forward_shift = noise(seeds[11], (D,), 0.3, 1.75, ((0, 16),))
    expand_weight = noise(seeds[12], (D, FF), D ** -0.5, 0.1875, ((0, 16), (1, 2)))
    expand_bias = noise(seeds[13], (FF,), 0.5, 3.0, ((0, 16),))
    reduce_weight = noise(seeds[14], (D, FF), (FF // 4) ** -0.5, 0.1875, ((0, 16), (1, 2)))
    reduce_bias = noise(seeds[15], (D,), 0.3, 1.75, ((0, 16),))
    forward_scale = jnp.clip(1.0 + 0.15 * jax.random.normal(seeds[16], (D,), jnp.float32), 0.25, 1.75).astype(jnp.bfloat16)
    return dict(tokens=tokens, cotangent=cotangent, attention_gain=attention_gain, attention_shift=attention_shift, triple_weight=triple_weight, query_bias=query_bias, value_bias=value_bias, merge_weight=merge_weight, merge_bias=merge_bias, attention_scale=attention_scale, forward_gain=forward_gain, forward_shift=forward_shift, expand_weight=expand_weight, expand_bias=expand_bias, reduce_weight=reduce_weight, reduce_bias=reduce_bias, forward_scale=forward_scale)


@jax.custom_vjp
def low(v):
    return lax.optimization_barrier(v.astype(jnp.bfloat16)).astype(jnp.float32)

@jax.custom_vjp
def low_back(v):
    return v

def low_keep(v):
    return (low(v), None)

def low_pass(kept, grad):
    return (grad,)

def back_keep(v):
    return (v, None)

def back_low(kept, grad):
    return (low(grad),)
low.defvjp(low_keep, low_pass)
low_back.defvjp(back_keep, back_low)

def layer_norm(values, gain, shift):
    centre = lax.optimization_barrier(jnp.mean(values, axis=-1, keepdims=True))
    centred = values - centre
    spread = lax.optimization_barrier(jnp.mean(centred * centred, axis=-1, keepdims=True))
    return centred * lax.rsqrt(spread + 1e-06) * gain + shift

def attend(block):
    queries, keys, values = block
    scores = jnp.einsum('qhd,khd->hqk', queries, keys, precision=lax.Precision.HIGHEST) * HD ** (-0.5)
    scores = low_back(scores)
    probs = low(jax.nn.softmax(scores, axis=-1))
    return jnp.einsum('hqk,khd->qhd', probs, values, precision=lax.Precision.HIGHEST)

def forward(inputs, attention_gain, attention_shift, triple_weight, query_bias, value_bias, merge_weight, merge_bias, attention_scale, forward_gain, forward_shift, expand_weight, expand_bias, reduce_weight, reduce_bias, forward_scale):
    rows = inputs.shape[0]
    images = rows // SEQ
    normed_one = low(layer_norm(inputs, attention_gain, attention_shift))
    triple = jnp.einsum('rd,dcf->rcf', normed_one, triple_weight, precision=lax.Precision.HIGHEST)
    bias_rows = jnp.stack([query_bias, jnp.zeros_like(query_bias), value_bias])
    triple = low(low_back(triple + bias_rows))
    shaped = triple.reshape(images, SEQ, 3, H, HD)
    mixed = lax.map(jax.checkpoint(attend), (shaped[:, :, 0], shaped[:, :, 1], shaped[:, :, 2]))
    mixed = low(low_back(mixed.reshape(rows, D)))
    attention_out = jnp.dot(mixed, merge_weight.T, precision=lax.Precision.HIGHEST, preferred_element_type=jnp.float32)
    branch_one = low_back(attention_out) + merge_bias
    middle = inputs + attention_scale * branch_one
    normed_two = low(layer_norm(middle, forward_gain, forward_shift))
    gate_input = jnp.dot(normed_two, expand_weight, precision=lax.Precision.HIGHEST, preferred_element_type=jnp.float32)
    gate_input = low_back(gate_input + expand_bias)
    activated = low(jax.nn.gelu(gate_input, approximate=False))
    forward_out = jnp.dot(activated, reduce_weight.T, precision=lax.Precision.HIGHEST, preferred_element_type=jnp.float32)
    branch_two = low_back(forward_out) + reduce_bias
    return middle + forward_scale * branch_two

def reference(tokens, cotangent, attention_gain, attention_shift, triple_weight, query_bias, value_bias, merge_weight, merge_bias, attention_scale, forward_gain, forward_shift, expand_weight, expand_bias, reduce_weight, reduce_bias, forward_scale):
    params = tuple((weight.astype(jnp.float32) for weight in (attention_gain, attention_shift, triple_weight, query_bias, value_bias, merge_weight, merge_bias, attention_scale, forward_gain, forward_shift, expand_weight, expand_bias, reduce_weight, reduce_bias, forward_scale)))
    inputs = tokens.astype(jnp.float32).reshape(-1, 2 * SEQ, D)
    upstream = cotangent.astype(jnp.float32).reshape(-1, 2 * SEQ, D)

    def step(totals, pair):
        block, back = pair
        output, pull = jax.vjp(forward, block, *params)
        grads = pull(back)
        totals = tuple((total + grad for total, grad in zip(totals, grads[1:])))
        return (totals, (output.astype(jnp.bfloat16), grads[0].astype(jnp.bfloat16)))
    zeros = tuple((jnp.zeros(weight.shape, jnp.float32) for weight in params))
    totals, (outputs, input_grads) = lax.scan(step, zeros, (inputs, upstream))
    return (outputs.reshape(-1, D), input_grads.reshape(-1, D), totals[0], totals[1], totals[2], totals[3], totals[4], totals[5], totals[6], totals[7], totals[8], totals[9], totals[10], totals[11], totals[12], totals[13], totals[14])
```

```python
import functools

import jax
import jax.numpy as jnp
from jax import lax
from jax.experimental import pallas as pl
from jax.experimental.pallas import tpu as pltpu
from jax.sharding import PartitionSpec as P

HD = 64
SEQ = 1370
PAIR = 128
F32 = jnp.float32
BF16 = jnp.bfloat16
FACTOR = HD ** (-0.5)
FACTOR_2 = FACTOR * 1.4426950408889634
VMEM = 56 * 2**20


def dot(left, right, left_dim, right_dim):
    dims = (((left_dim,), (right_dim,)), ((), ()))
    return lax.dot_general(left, right, dims, preferred_element_type=F32)


class Tree:
    def __init__(self, mesh):
        self.dp = mesh.shape["dp"]
        self.tensor = mesh.shape["tensor"]
        dp_bits = self.dp.bit_length() - 1
        tensor_bits = self.tensor.bit_length() - 1
        if 1 << dp_bits != self.dp or 1 << tensor_bits != self.tensor or dp_bits < 2:
            raise ValueError("mesh sizes")
        high = [("dp", bit) for bit in range(dp_bits - 1, 1, -1)]
        tensor_stages = [("tensor", bit) for bit in range(tensor_bits - 1, -1, -1)]
        self.orders = (
            high + [("dp", 1)] + tensor_stages,
            high + tensor_stages + [("dp", 1)],
        )
        self.half_blocks = self.dp * self.tensor // 2

    def swap(self, value, stage):
        axis, bit = stage
        size = self.dp if axis == "dp" else self.tensor
        return lax.ppermute(value, axis, [(i, i ^ (1 << bit)) for i in range(size)])

    def tables(self):
        me_dp = lax.axis_index("dp")
        me_tensor = lax.axis_index("tensor")
        place = jnp.arange(self.half_blocks, dtype=jnp.int32)
        pairs = self.dp // 2
        relative = {
            "dp": ((place % pairs) << 1) ^ (me_dp & ~1),
            "tensor": (place // pairs) ^ me_tensor,
        }
        rows = []
        for order in self.orders:
            index = jnp.zeros_like(place)
            for position, (axis, bit) in enumerate(order):
                index = index + (((relative[axis] >> bit) & 1) << position)
            rows.append(index)
        core = jnp.full_like(place, me_dp & 1)
        return jnp.stack(rows + [core]).astype(jnp.int32)

    def gather(self, shard, tables, widths):
        rows, width = shard.shape
        half = rows // 2
        pieces = []
        for order, start in zip(self.orders, (0, half)):
            held = shard[start : start + half][None]
            for stage in order:
                held = jnp.concatenate([held, self.swap(held, stage)], axis=0)
            pieces += [held, self.swap(held, ("dp", 0))]
        return self.assemble(pieces, tables, half, widths)

    def assemble(self, pieces, tables, half, widths):
        pairs = self.dp // 2
        total = sum(widths)

        def kernel(tables_ref, own_a, far_a, own_b, far_b, *outs):
            core = tables_ref[2, 0]

            def put(first_a, second_a, first_b, second_b):
                at = 0
                for out, width in zip(outs, widths):
                    columns = slice(at, at + width)
                    out[0:half] = first_a[:, columns]
                    out[half : 2 * half] = first_b[:, columns]
                    out[2 * half : 3 * half] = second_a[:, columns]
                    out[3 * half : 4 * half] = second_b[:, columns]
                    at += width

            @pl.when(core == 0)
            def _():
                put(own_a, far_a, own_b, far_b)

            @pl.when(core != 0)
            def _():
                put(far_a, own_a, far_b, own_b)

        spec_a = pl.BlockSpec((None, half, total), lambda i, table: (table[0, i], 0, 0))
        spec_b = pl.BlockSpec((None, half, total), lambda i, table: (table[1, i], 0, 0))
        return pl.pallas_call(
            kernel,
            grid_spec=pltpu.PrefetchScalarGridSpec(
                num_scalar_prefetch=1,
                grid=(self.half_blocks,),
                in_specs=[spec_a, spec_a, spec_b, spec_b],
                out_specs=[
                    pl.BlockSpec((4 * half, width), lambda i, table: (i % pairs, i // pairs))
                    for width in widths
                ],
            ),
            out_shape=[
                jax.ShapeDtypeStruct((self.dp * 2 * half, self.tensor * width), BF16)
                for width in widths
            ],
            compiler_params=pltpu.CompilerParams(vmem_limit_bytes=VMEM),
        )(tables, *pieces)

    def split(self, arrays, tables, half, widths):
        pairs = self.dp // 2
        total = sum(widths)

        def kernel(tables_ref, *refs):
            sources, (own_a, far_a, own_b, far_b) = refs[: len(widths)], refs[len(widths) :]
            core = tables_ref[2, 0]

            def take(first_a, second_a, first_b, second_b):
                at = 0
                for source, width in zip(sources, widths):
                    columns = slice(at, at + width)
                    first_a[:, columns] = source[0:half]
                    first_b[:, columns] = source[half : 2 * half]
                    second_a[:, columns] = source[2 * half : 3 * half]
                    second_b[:, columns] = source[3 * half : 4 * half]
                    at += width

            @pl.when(core == 0)
            def _():
                take(own_a, far_a, own_b, far_b)

            @pl.when(core != 0)
            def _():
                take(far_a, own_a, far_b, own_b)

        spec_a = pl.BlockSpec((None, half, total), lambda i, table: (table[0, i], 0, 0))
        spec_b = pl.BlockSpec((None, half, total), lambda i, table: (table[1, i], 0, 0))
        shape = jax.ShapeDtypeStruct((self.half_blocks, half, total), BF16)
        return pl.pallas_call(
            kernel,
            grid_spec=pltpu.PrefetchScalarGridSpec(
                num_scalar_prefetch=1,
                grid=(self.half_blocks,),
                in_specs=[
                    pl.BlockSpec((4 * half, width), lambda i, table: (i % pairs, i // pairs))
                    for width in widths
                ],
                out_specs=[spec_a, spec_a, spec_b, spec_b],
            ),
            out_shape=[shape] * 4,
            compiler_params=pltpu.CompilerParams(vmem_limit_bytes=VMEM),
        )(tables, *arrays)

    def scatter(self, arrays, tables):
        rows = arrays[0].shape[0] // self.dp
        widths = [array.shape[1] // self.tensor for array in arrays]
        own_a, far_a, own_b, far_b = self.split(arrays, tables, rows // 2, widths)
        halves = []
        for order, own, far in zip(self.orders, (own_a, own_b), (far_a, far_b)):
            held, sent = own, far
            stages = [("dp", 0)] + order[::-1]
            for number, stage in enumerate(stages):
                held = held.astype(F32) + self.swap(sent, stage).astype(F32)
                if number + 1 < len(stages):
                    held = held.astype(BF16)
                    middle = held.shape[0] // 2
                    held, sent = held[:middle], held[middle:]
            halves.append(held[0])
        whole = jnp.concatenate(halves, axis=0)
        parts, at = [], 0
        for width in widths:
            parts.append(whole[:, at : at + width])
            at += width
        return parts

    def gather_rows(self, row):
        held = row[None]
        bits = range(self.dp.bit_length() - 2, -1, -1)
        for bit in bits:
            held = jnp.concatenate([self.swap(held, ("dp", bit)), held], axis=0)
        index = self.row_index()
        return held[index]

    def row_index(self):
        bits = self.dp.bit_length() - 1
        relative = jnp.arange(self.dp) ^ lax.axis_index("dp")
        index = jnp.zeros_like(relative)
        for position, bit in enumerate(range(bits - 1, -1, -1)):
            index = index + ((1 - ((relative >> bit) & 1)) << position)
        return index

    def scatter_rows(self, rows):
        relative = rows[jnp.arange(self.dp) ^ lax.axis_index("dp")]
        held = relative
        for bit in range(self.tensor.bit_length() - 1):
            held = held + self.swap(held, ("tensor", bit))
        for bit in range(self.dp.bit_length() - 2, -1, -1):
            middle = held.shape[0] // 2
            held = held[:middle] + self.swap(held[middle:], ("dp", bit))
        return held[0]


def split_pair(block):
    lane = lax.broadcasted_iota(jnp.int32, block.shape, 1)
    zero = jnp.zeros_like(block)
    return jnp.concatenate(
        [jnp.where(lane < HD, block, zero), jnp.where(lane >= HD, block, zero)], axis=0
    )


def join_pair(block):
    rows = block.shape[0] // 2
    lane = lax.broadcasted_iota(jnp.int32, (rows, PAIR), 1)
    return jnp.where(lane < HD, block[:rows], block[rows:])


def mask_keys(scores, segment, valid, fill):
    if valid == segment:
        return scores
    start = valid // 128 * 128
    parts = []
    for base in range(0, scores.shape[1], segment):
        if start:
            parts.append(scores[:, base : base + start])
        tail = scores[:, base + start : base + segment]
        lane = lax.broadcasted_iota(jnp.int32, tail.shape, 1) + start
        parts.append(jnp.where(lane < valid, tail, fill))
    return jnp.concatenate(parts, axis=1)


def attend_forward_kernel(segment, valid, query_ref, pair_ref, mixed_ref, logsum_ref, value_ref):
    keys = pair_ref.at[:, PAIR : 2 * PAIR]
    value_ref[:, 0:PAIR] = pair_ref[:, 2 * PAIR : 3 * PAIR]
    value_ref[:, PAIR : 2 * PAIR] = jnp.ones((value_ref.shape[0], PAIR), BF16)
    for chunk in range(query_ref.shape[0] // 128):
        rows = pl.ds(chunk * 128, 128)
        queries = split_pair(query_ref[rows, 0:PAIR])
        scores = mask_keys(dot(queries, keys[...], 1, 1), segment, valid, -1e30)
        peak = jnp.max(scores, axis=1, keepdims=True)
        weights = jnp.exp2((scores - peak) * FACTOR_2).astype(BF16)
        mixed = dot(weights, value_ref[...], 1, 0)
        total = mixed[:, PAIR:]
        mixed_ref[rows, :] = join_pair(mixed[:, :PAIR] / total).astype(BF16)
        logsum_ref[rows, :] = join_pair(peak * FACTOR_2 + jnp.log2(total))


def attend_backward_kernel(
    segment, valid, joint, query_ref, pair_ref, mixed_ref, grad_ref, logsum_ref, *rest
):
    if joint:
        out_ref, key_sum, value_sum = rest
        query_out = out_ref.at[:, 0:PAIR]
        key_out = out_ref.at[:, PAIR : 2 * PAIR]
        value_out = out_ref.at[:, 2 * PAIR : 3 * PAIR]
    else:
        query_out, pair_out, key_sum, value_sum = rest
        key_out = pair_out.at[:, 0:PAIR]
        value_out = pair_out.at[:, PAIR : 2 * PAIR]
    keys = pair_ref.at[:, PAIR : 2 * PAIR]
    values = pair_ref.at[:, 2 * PAIR : 3 * PAIR]
    key_total = value_total = None
    for chunk in range(query_ref.shape[0] // 128):
        rows = pl.ds(chunk * 128, 128)
        queries = split_pair(query_ref[rows, 0:PAIR])
        grad = grad_ref[rows, :]
        grads = split_pair(grad)
        row_term = jnp.sum(
            split_pair(grad.astype(F32) * mixed_ref[rows, :].astype(F32)), axis=1, keepdims=True
        )
        logsum = logsum_ref[rows, :]
        logsum = jnp.concatenate([logsum[:, 0:1], logsum[:, HD : HD + 1]], axis=0)
        scores = dot(queries, keys[...], 1, 1)
        probs = mask_keys(jnp.exp2(scores * FACTOR_2 - logsum), segment, valid, 0.0)
        prob_grad = dot(grads, values[...], 1, 1)
        score_grad = (probs * (prob_grad - row_term)).astype(BF16)
        query_grad = join_pair(dot(score_grad, keys[...], 1, 0)) * FACTOR
        query_out[rows, :] = query_grad.astype(BF16)
        value_part = dot(grads.T, probs.astype(BF16), 1, 0)
        key_part = dot(queries.T, score_grad, 1, 0)
        if chunk == 0:
            value_sum[...] = value_part
            key_sum[...] = key_part
        else:
            value_sum[...] += value_part
            key_sum[...] += key_part
    key_out[...] = (key_sum[...] * FACTOR).T.astype(BF16)
    value_out[...] = value_sum[...].T.astype(BF16)


def attend_cost(products, images, pairs, rows, key_rows):
    area = images * pairs * 2 * rows * key_rows
    return pl.CostEstimate(
        flops=2 * products * area * HD * 4,
        bytes_accessed=images * pairs * rows * PAIR * 16,
        transcendentals=area,
    )


def attend_forward(triple, gathered, segment, valid):
    images, rows, width = triple.shape
    key_rows = gathered.shape[1]
    pairs = width // (3 * PAIR)
    at = lambda i, g: (i, 0, g)
    return pl.pallas_call(
        functools.partial(attend_forward_kernel, segment, valid),
        grid=(images, pairs),
        in_specs=[
            pl.BlockSpec((None, rows, 3 * PAIR), at),
            pl.BlockSpec((None, key_rows, 3 * PAIR), at),
        ],
        out_specs=[
            pl.BlockSpec((None, rows, PAIR), at),
            pl.BlockSpec((None, rows, PAIR), at),
        ],
        out_shape=[
            jax.ShapeDtypeStruct((images, rows, pairs * PAIR), BF16),
            jax.ShapeDtypeStruct((images, rows, pairs * PAIR), F32),
        ],
        scratch_shapes=[pltpu.VMEM((key_rows, 2 * PAIR), BF16)],
        cost_estimate=attend_cost(2, images, pairs, rows, key_rows),
        compiler_params=pltpu.CompilerParams(vmem_limit_bytes=VMEM),
    )(triple, gathered)


def attend_backward(triple, gathered, mixed, mixed_grad, logsum, segment, valid):
    images, rows, width = triple.shape
    key_rows = gathered.shape[1]
    pairs = width // (3 * PAIR)
    joint = key_rows == rows
    at = lambda i, g: (i, 0, g)
    row_spec = pl.BlockSpec((None, rows, PAIR), at)
    triple_spec = pl.BlockSpec((None, rows, 3 * PAIR), at)
    if joint:
        out_specs = [triple_spec]
        out_shape = [jax.ShapeDtypeStruct(triple.shape, BF16)]
    else:
        out_specs = [row_spec, pl.BlockSpec((None, key_rows, 2 * PAIR), at)]
        out_shape = [
            jax.ShapeDtypeStruct((images, rows, pairs * PAIR), BF16),
            jax.ShapeDtypeStruct((images, key_rows, pairs * 2 * PAIR), BF16),
        ]
    outs = pl.pallas_call(
        functools.partial(attend_backward_kernel, segment, valid, joint),
        grid=(images, pairs),
        in_specs=[
            triple_spec,
            pl.BlockSpec((None, key_rows, 3 * PAIR), at),
            row_spec,
            row_spec,
            row_spec,
        ],
        out_specs=out_specs,
        out_shape=out_shape,
        scratch_shapes=[pltpu.VMEM((PAIR, key_rows), F32)] * 2,
        cost_estimate=attend_cost(5, images, pairs, rows, key_rows),
        compiler_params=pltpu.CompilerParams(vmem_limit_bytes=VMEM),
    )(triple, gathered, mixed, mixed_grad, logsum)
    if joint:
        return outs[0]
    query_grad, pair_grad = outs
    shares = key_rows // rows
    tensor = lax.axis_size("tensor")
    groups = [list(range(base, base + shares)) for base in range(0, tensor, shares)]
    pair_grad = lax.psum_scatter(
        pair_grad, "tensor", scatter_dimension=1, axis_index_groups=groups, tiled=True
    )
    return jnp.concatenate(
        [
            query_grad.reshape(images, rows, pairs, PAIR),
            pair_grad.reshape(images, rows, pairs, 2 * PAIR),
        ],
        axis=3,
    ).reshape(images, rows, width)


def norm_parts(values):
    centre = jnp.mean(values, axis=-1, keepdims=True)
    centred = values - centre
    spread = jnp.mean(centred * centred, axis=-1, keepdims=True)
    inverse = lax.rsqrt(spread + 1e-06)
    return centred * inverse, inverse


def norm_backward(grad, gain, normed, inverse):
    scaled = grad * gain
    return inverse * (
        scaled
        - jnp.mean(scaled, axis=-1, keepdims=True)
        - normed * jnp.mean(scaled * normed, axis=-1, keepdims=True)
    )


def gelu_parts(values):
    below = 0.5 * lax.erfc(-values * (0.5**0.5))
    density = jnp.exp(-0.5 * values * values) * 0.3989422804014327
    return values * below, below + values * density


def body(
    mesh,
    tokens,
    cotangent,
    attention_gain,
    attention_shift,
    triple_weight,
    query_bias,
    value_bias,
    merge_weight,
    merge_bias,
    attention_scale,
    forward_gain,
    forward_shift,
    expand_weight,
    expand_bias,
    reduce_weight,
    reduce_bias,
    forward_scale,
):
    tree = Tree(mesh)
    tables = tree.tables()
    count, width = tokens.shape
    segment_rows = min(count, SEQ)
    images = count // segment_rows
    shares = SEQ // segment_rows
    if images * segment_rows != count or shares * segment_rows != SEQ:
        raise ValueError("token rows")
    padded = -(-segment_rows // 128) * 128
    rows = images * padded

    def pad(values):
        shaped = values.reshape(images, segment_rows, width)
        shaped = jnp.pad(shaped, ((0, 0), (0, padded - segment_rows), (0, 0)))
        return shaped.reshape(rows, width)

    def unpad(values):
        return values.reshape(images, padded, width)[:, :segment_rows].reshape(count, width)

    vectors = [
        attention_gain,
        attention_shift,
        query_bias,
        value_bias,
        merge_bias,
        attention_scale,
        forward_gain,
        forward_shift,
        reduce_bias,
        forward_scale,
        expand_bias,
    ]
    sizes = [vector.shape[0] for vector in vectors]
    packed = jnp.concatenate(vectors)
    extent = -(-packed.shape[0] // 1024) * 1024
    packed = jnp.pad(packed, (0, extent - packed.shape[0])).astype(F32)
    gathered = tree.gather_rows(packed.reshape(-1, 128)).reshape(tree.dp, extent)
    full, at = [], 0
    for size in sizes:
        full.append(gathered[:, at : at + size].reshape(-1))
        at += size
    (
        gain_one,
        shift_one,
        query_shift,
        value_shift,
        merge_shift,
        scale_one,
        gain_two,
        shift_two,
        reduce_shift,
        scale_two,
        expand_shift,
    ) = full

    shard_rows, _, local = triple_weight.shape
    local_pairs = local // PAIR
    triple_shard = (
        triple_weight.reshape(shard_rows, 3, local_pairs, PAIR)
        .transpose(0, 2, 1, 3)
        .reshape(shard_rows, 3 * local)
    )
    (triple_full,) = tree.gather(triple_shard, tables, [3 * local])
    widths = [merge_weight.shape[1], expand_weight.shape[1], reduce_weight.shape[1]]
    merge_full, expand_full, reduce_full = tree.gather(
        jnp.concatenate([merge_weight, expand_weight, reduce_weight], axis=1), tables, widths
    )

    inputs = pad(tokens).astype(F32)
    normal_one, inverse_one = norm_parts(inputs)
    normed_one = (normal_one * gain_one + shift_one).astype(BF16)
    pairs = tree.tensor * local_pairs
    bias = jnp.stack(
        [
            query_shift.reshape(pairs, PAIR),
            jnp.zeros((pairs, PAIR), F32),
            value_shift.reshape(pairs, PAIR),
        ],
        axis=1,
    ).reshape(-1)
    triple = (dot(normed_one, triple_full, 1, 0) + bias).astype(BF16)
    triple = triple.reshape(images, padded, -1)
    pair_rows = triple
    if shares > 1:
        groups = [list(range(base, base + shares)) for base in range(0, tree.tensor, shares)]
        pair_rows = lax.all_gather(
            triple, "tensor", axis=1, axis_index_groups=groups, tiled=True
        )
    mixed, logsum = attend_forward(triple, pair_rows, padded, segment_rows)
    mixed_rows = mixed.reshape(rows, width)
    branch_one = dot(mixed_rows, merge_full, 1, 1) + merge_shift
    middle = inputs + scale_one * branch_one
    normal_two, inverse_two = norm_parts(middle)
    normed_two = (normal_two * gain_two + shift_two).astype(BF16)

    upstream = pad(cotangent).astype(F32)
    back_two = (upstream * scale_two).astype(BF16)
    gate_input = dot(normed_two, expand_full, 1, 0) + expand_shift
    activated, slope = gelu_parts(gate_input)
    activated = activated.astype(BF16)
    slope = slope.astype(BF16)
    gate_grad = (dot(back_two, reduce_full, 1, 0) * slope.astype(F32)).astype(BF16)
    branch_two = dot(activated, reduce_full, 1, 1) + reduce_shift
    result = unpad((middle + scale_two * branch_two).astype(BF16))
    reduce_grad = dot(back_two, activated, 0, 0).astype(BF16)
    expand_grad = dot(normed_two, gate_grad, 0, 0).astype(BF16)
    expand_out, reduce_out = tree.scatter([expand_grad, reduce_grad], tables)
    normed_two_grad = dot(gate_grad, expand_full, 1, 1)

    middle_grad = upstream + norm_backward(normed_two_grad, gain_two, normal_two, inverse_two)
    back_one = (middle_grad * scale_one).astype(BF16)
    mixed_grad = dot(back_one, merge_full, 1, 0).astype(BF16).reshape(images, padded, width)
    merge_grad = dot(back_one, mixed_rows, 0, 0).astype(BF16)
    (merge_out,) = tree.scatter([merge_grad], tables)
    triple_grad = attend_backward(
        triple, pair_rows, mixed, mixed_grad, logsum, padded, segment_rows
    )
    triple_grad = triple_grad.reshape(rows, -1)
    weight_grad = dot(normed_one, triple_grad, 0, 0).astype(BF16)
    (triple_out,) = tree.scatter([weight_grad], tables)
    triple_out = (
        triple_out.reshape(shard_rows, local_pairs, 3, PAIR)
        .transpose(0, 2, 1, 3)
        .reshape(shard_rows, 3, local)
    )
    normed_one_grad = dot(triple_grad, triple_full, 1, 1)
    tokens_grad = middle_grad + norm_backward(normed_one_grad, gain_one, normal_one, inverse_one)
    tokens_grad = unpad(tokens_grad.astype(BF16))

    bias_sums = jnp.sum(triple_grad, axis=0, dtype=F32).reshape(pairs, 3, PAIR)
    sums = [
        jnp.sum(normed_one_grad * normal_one, axis=0),
        jnp.sum(normed_one_grad, axis=0),
        bias_sums[:, 0].reshape(-1),
        bias_sums[:, 2].reshape(-1),
        jnp.sum(middle_grad, axis=0) * scale_one,
        jnp.sum(middle_grad * branch_one, axis=0),
        jnp.sum(normed_two_grad * normal_two, axis=0),
        jnp.sum(normed_two_grad, axis=0),
        jnp.sum(upstream, axis=0) * scale_two,
        jnp.sum(upstream * branch_two, axis=0),
        jnp.sum(gate_grad, axis=0, dtype=F32),
    ]
    columns = jnp.concatenate([total.reshape(tree.dp, -1) for total in sums], axis=1)
    columns = jnp.pad(columns, ((0, 0), (0, extent - columns.shape[1])))
    mine = tree.scatter_rows(columns.reshape(tree.dp, -1, 128)).reshape(-1)
    vector_out, at = [], 0
    for size in sizes:
        vector_out.append(mine[at : at + size])
        at += size
    return (
        result,
        tokens_grad,
        vector_out[0],
        vector_out[1],
        triple_out,
        vector_out[2],
        vector_out[3],
        merge_out,
        vector_out[4],
        vector_out[5],
        vector_out[6],
        vector_out[7],
        expand_out,
        vector_out[10],
        reduce_out,
        vector_out[8],
        vector_out[9],
    )


def solution(mesh):
    rows = P(("dp", "tensor"), None)
    vector = P("dp")
    weight = P("dp", "tensor")
    triple = P("dp", None, "tensor")
    parameters = (
        vector,
        vector,
        triple,
        vector,
        vector,
        weight,
        vector,
        vector,
        vector,
        vector,
        weight,
        vector,
        weight,
        vector,
        vector,
    )
    return jax.shard_map(
        functools.partial(body, mesh),
        mesh=mesh,
        in_specs=(rows, rows) + parameters,
        out_specs=(rows, rows) + parameters,
        check_vma=False,
    )
```

```python
import functools

import jax
import jax.numpy as jnp
from jax import lax
from jax.experimental import pallas as pl
from jax.experimental.pallas import tpu as pltpu
from jax.sharding import PartitionSpec as P

HD = 64
SEQ = 1370
PAIR = 128
F32 = jnp.float32
BF16 = jnp.bfloat16
FACTOR = HD ** (-0.5)
FACTOR_2 = FACTOR * 1.4426950408889634
VMEM = 56 * 2**20


def dot(left, right, left_dim, right_dim):
    dims = (((left_dim,), (right_dim,)), ((), ()))
    return lax.dot_general(left, right, dims, preferred_element_type=F32)


class Tree:
    def __init__(self, mesh):
        self.dp = mesh.shape["dp"]
        self.tensor = mesh.shape["tensor"]
        dp_bits = self.dp.bit_length() - 1
        tensor_bits = self.tensor.bit_length() - 1
        if 1 << dp_bits != self.dp or 1 << tensor_bits != self.tensor or dp_bits < 2:
            raise ValueError("mesh sizes")
        high = [("dp", tuple(range(dp_bits - 1, 1, -1)))]
        tensor_stages = [("tensor", (bit,)) for bit in range(tensor_bits - 1, -1, -1)]
        self.orders = (
            high + [("dp", (1,))] + tensor_stages,
            high + tensor_stages + [("dp", (1,))],
        )
        self.half_blocks = self.dp * self.tensor // 2

    def masks(self, stage):
        bits = stage[1]
        return [
            sum(1 << bit for place, bit in enumerate(bits) if choice >> place & 1)
            for choice in range(1, 1 << len(bits))
        ]

    def swap(self, value, axis, mask):
        size = self.dp if axis == "dp" else self.tensor
        return lax.ppermute(value, axis, [(i, i ^ mask) for i in range(size)])

    def spread(self, held, stage):
        return jnp.concatenate(
            [held] + [self.swap(held, stage[0], mask) for mask in self.masks(stage)], axis=0
        )

    def add_up(self, held, stage):
        size = held.shape[0] >> len(stage[1])
        total = held[:size]
        for place, mask in enumerate(self.masks(stage), 1):
            total = total + self.swap(held[place * size : (place + 1) * size], stage[0], mask)
        return total

    def tables(self):
        me_dp = lax.axis_index("dp")
        me_tensor = lax.axis_index("tensor")
        place = jnp.arange(self.half_blocks, dtype=jnp.int32)
        pairs = self.dp // 2
        relative = {
            "dp": ((place % pairs) << 1) ^ (me_dp & ~1),
            "tensor": (place // pairs) ^ me_tensor,
        }
        rows = []
        for order in self.orders:
            index = jnp.zeros_like(place)
            flat = [(axis, bit) for axis, bits in order for bit in bits]
            for position, (axis, bit) in enumerate(flat):
                index = index + (((relative[axis] >> bit) & 1) << position)
            rows.append(index)
        core = jnp.full_like(place, me_dp & 1)
        return jnp.stack(rows + [core]).astype(jnp.int32)

    def gather(self, shard):
        half = shard.shape[0] // 2
        return Gather(self, [shard[:half][None], shard[half:][None]])

    def assemble(self, pieces, tables, half, widths):
        pairs = self.dp // 2
        total = sum(widths)
        if 4 * half * self.half_blocks * total < 5 * 2**20:
            return self.assemble_whole(pieces, tables, half, widths)

        def kernel(tables_ref, own_a, far_a, own_b, far_b, *outs):
            core = tables_ref[2, 0]

            def put(first_a, second_a, first_b, second_b):
                at = 0
                for out, width in zip(outs, widths):
                    columns = slice(at, at + width)
                    out[0:half] = first_a[:, columns]
                    out[half : 2 * half] = first_b[:, columns]
                    out[2 * half : 3 * half] = second_a[:, columns]
                    out[3 * half : 4 * half] = second_b[:, columns]
                    at += width

            @pl.when(core == 0)
            def _():
                put(own_a, far_a, own_b, far_b)

            @pl.when(core != 0)
            def _():
                put(far_a, own_a, far_b, own_b)

        spec_a = pl.BlockSpec((None, half, total), lambda i, table: (table[0, i], 0, 0))
        spec_b = pl.BlockSpec((None, half, total), lambda i, table: (table[1, i], 0, 0))
        return pl.pallas_call(
            kernel,
            grid_spec=pltpu.PrefetchScalarGridSpec(
                num_scalar_prefetch=1,
                grid=(self.half_blocks,),
                in_specs=[spec_a, spec_a, spec_b, spec_b],
                out_specs=[
                    pl.BlockSpec((4 * half, width), lambda i, table: (i % pairs, i // pairs))
                    for width in widths
                ],
            ),
            out_shape=[
                jax.ShapeDtypeStruct((self.dp * 2 * half, self.tensor * width), BF16)
                for width in widths
            ],
            compiler_params=pltpu.CompilerParams(vmem_limit_bytes=VMEM),
        )(tables, *pieces)

    def assemble_whole(self, pieces, tables, half, widths):
        pairs = self.dp // 2

        def kernel(tables_ref, own_a, far_a, own_b, far_b, *outs):
            core = tables_ref[2, 0]

            @pl.loop(0, pairs)
            def _(pair):
                own = pl.multiple_of((2 * pair + core) * 2 * half, 2 * half)
                far = pl.multiple_of((2 * pair + 1 - core) * 2 * half, 2 * half)
                for tensor in range(self.tensor):
                    at_a = tables_ref[0, tensor * pairs + pair]
                    at_b = tables_ref[1, tensor * pairs + pair]
                    at = 0
                    for out, width in zip(outs, widths):
                        source = slice(at, at + width)
                        columns = slice(tensor * width, (tensor + 1) * width)
                        out[pl.ds(own, half), columns] = own_a[at_a, :, source]
                        out[pl.ds(own + half, half), columns] = own_b[at_b, :, source]
                        out[pl.ds(far, half), columns] = far_a[at_a, :, source]
                        out[pl.ds(far + half, half), columns] = far_b[at_b, :, source]
                        at += width

        return self.whole_call(
            kernel,
            tables,
            pieces,
            [(self.dp * 2 * half, self.tensor * width) for width in widths],
        )

    def split_whole(self, arrays, tables, half, widths):
        pairs = self.dp // 2

        def kernel(tables_ref, *refs):
            sources, (own_a, far_a, own_b, far_b) = refs[: len(widths)], refs[len(widths) :]
            core = tables_ref[2, 0]

            @pl.loop(0, pairs)
            def _(pair):
                own = pl.multiple_of((2 * pair + core) * 2 * half, 2 * half)
                far = pl.multiple_of((2 * pair + 1 - core) * 2 * half, 2 * half)
                for tensor in range(self.tensor):
                    at_a = tables_ref[0, tensor * pairs + pair]
                    at_b = tables_ref[1, tensor * pairs + pair]
                    at = 0
                    for source, width in zip(sources, widths):
                        target = slice(at, at + width)
                        columns = slice(tensor * width, (tensor + 1) * width)
                        own_a[at_a, :, target] = source[pl.ds(own, half), columns]
                        own_b[at_b, :, target] = source[pl.ds(own + half, half), columns]
                        far_a[at_a, :, target] = source[pl.ds(far, half), columns]
                        far_b[at_b, :, target] = source[pl.ds(far + half, half), columns]
                        at += width

        return self.whole_call(
            kernel, tables, arrays, [(self.half_blocks, half, sum(widths))] * 4
        )

    def whole_call(self, kernel, tables, values, shapes):
        vmem = pl.BlockSpec(memory_space=pltpu.VMEM)
        return pl.pallas_call(
            kernel,
            in_specs=[pl.BlockSpec(memory_space=pltpu.SMEM)] + [vmem] * len(values),
            out_specs=[vmem] * len(shapes),
            out_shape=[jax.ShapeDtypeStruct(shape, BF16) for shape in shapes],
            compiler_params=pltpu.CompilerParams(vmem_limit_bytes=VMEM),
        )(tables, *values)

    def split(self, arrays, tables, half, widths):
        pairs = self.dp // 2
        total = sum(widths)
        if 4 * half * self.half_blocks * total < 5 * 2**20:
            return self.split_whole(arrays, tables, half, widths)

        def kernel(tables_ref, *refs):
            sources, (own_a, far_a, own_b, far_b) = refs[: len(widths)], refs[len(widths) :]
            core = tables_ref[2, 0]

            def take(first_a, second_a, first_b, second_b):
                at = 0
                for source, width in zip(sources, widths):
                    columns = slice(at, at + width)
                    first_a[:, columns] = source[0:half]
                    first_b[:, columns] = source[half : 2 * half]
                    second_a[:, columns] = source[2 * half : 3 * half]
                    second_b[:, columns] = source[3 * half : 4 * half]
                    at += width

            @pl.when(core == 0)
            def _():
                take(own_a, far_a, own_b, far_b)

            @pl.when(core != 0)
            def _():
                take(far_a, own_a, far_b, own_b)

        spec_a = pl.BlockSpec((None, half, total), lambda i, table: (table[0, i], 0, 0))
        spec_b = pl.BlockSpec((None, half, total), lambda i, table: (table[1, i], 0, 0))
        shape = jax.ShapeDtypeStruct((self.half_blocks, half, total), BF16)
        return pl.pallas_call(
            kernel,
            grid_spec=pltpu.PrefetchScalarGridSpec(
                num_scalar_prefetch=1,
                grid=(self.half_blocks,),
                in_specs=[
                    pl.BlockSpec((4 * half, width), lambda i, table: (i % pairs, i // pairs))
                    for width in widths
                ],
                out_specs=[spec_a, spec_a, spec_b, spec_b],
            ),
            out_shape=[shape] * 4,
            compiler_params=pltpu.CompilerParams(vmem_limit_bytes=VMEM),
        )(tables, *arrays)

    def scatter(self, arrays, tables):
        rows = arrays[0].shape[0] // self.dp
        widths = [array.shape[1] // self.tensor for array in arrays]
        return Scatter(self, self.split(arrays, tables, rows // 2, widths), widths)

    def row_stages(self):
        bits = tuple(range(self.dp.bit_length() - 1))
        return [("dp", bits[2:]), ("dp", bits[:2])]

    def gather_rows(self, row):
        held = row[None]
        stages = self.row_stages()
        for stage in stages:
            held = self.spread(held, stage)
        relative = jnp.arange(self.dp) ^ lax.axis_index("dp")
        index = jnp.zeros_like(relative)
        for position, bit in enumerate(bit for stage in stages for bit in stage[1]):
            index = index + (((relative >> bit) & 1) << position)
        return held[index]

    def scatter_rows(self, rows):
        stages = self.row_stages()
        place = jnp.arange(self.dp)
        relative = jnp.zeros_like(place)
        for position, bit in enumerate(bit for stage in stages for bit in stage[1]):
            relative = relative + (((place >> position) & 1) << bit)
        held = rows[relative ^ lax.axis_index("dp")]
        for bit in range(self.tensor.bit_length() - 1):
            held = held + self.swap(held, "tensor", 1 << bit)
        for stage in stages[::-1]:
            held = self.add_up(held, stage)
        return held[0]


class Gather:
    def __init__(self, tree, held):
        self.tree = tree
        self.held = held
        self.done = 0
        self.stages = len(tree.orders[0])

    def step(self):
        if self.done < self.stages:
            self.held = [
                self.tree.spread(held, order[self.done])
                for held, order in zip(self.held, self.tree.orders)
            ]
        elif self.done == self.stages:
            self.held = self.held + [self.tree.swap(held, "dp", 1) for held in self.held]
        self.done += 1

    def finish(self, tables, widths):
        while self.done <= self.stages:
            self.step()
        own_a, own_b, far_a, far_b = self.held
        half = own_a.shape[1]
        return self.tree.assemble([own_a, far_a, own_b, far_b], tables, half, widths)


class Scatter:
    def __init__(self, tree, pieces, widths):
        own_a, far_a, own_b, far_b = pieces
        self.tree = tree
        self.widths = widths
        self.held = [own_a, own_b]
        self.sent = [[far_a], [far_b]]
        self.orders = [[("dp", (0,))] + order[::-1] for order in tree.orders]
        self.done = 0

    def step(self):
        if self.done == len(self.orders[0]):
            return
        last = self.done + 1 == len(self.orders[0])
        for side, order in enumerate(self.orders):
            stage = order[self.done]
            held = self.held[side].astype(F32)
            for value, mask in zip(self.sent[side], self.tree.masks(stage)):
                held = held + self.tree.swap(value, stage[0], mask).astype(F32)
            if not last:
                held = held.astype(BF16)
                count = 1 << len(order[self.done + 1][1])
                size = held.shape[0] // count
                held, *self.sent[side] = [
                    held[place * size : (place + 1) * size] for place in range(count)
                ]
            self.held[side] = held
        self.done += 1

    def finish(self):
        while self.done < len(self.orders[0]):
            self.step()
        whole = jnp.concatenate([held[0] for held in self.held], axis=0)
        parts, at = [], 0
        for width in self.widths:
            parts.append(whole[:, at : at + width])
            at += width
        return parts


def after(value, *chains):
    waits = [(chain.held, getattr(chain, "sent", ())) for chain in chains]
    return lax.optimization_barrier((value, waits))[0]


def split_pair(block):
    lane = lax.broadcasted_iota(jnp.int32, block.shape, 1)
    zero = jnp.zeros_like(block)
    return jnp.concatenate(
        [jnp.where(lane < HD, block, zero), jnp.where(lane >= HD, block, zero)], axis=0
    )


def join_pair(block):
    rows = block.shape[0] // 2
    lane = lax.broadcasted_iota(jnp.int32, (rows, PAIR), 1)
    return jnp.where(lane < HD, block[:rows], block[rows:])


def mask_keys(scores, segment, valid, fill):
    if valid == segment:
        return scores
    start = valid // 128 * 128
    parts = []
    for base in range(0, scores.shape[1], segment):
        if start:
            parts.append(scores[:, base : base + start])
        tail = scores[:, base + start : base + segment]
        lane = lax.broadcasted_iota(jnp.int32, tail.shape, 1) + start
        parts.append(jnp.where(lane < valid, tail, fill))
    return jnp.concatenate(parts, axis=1)


def attend_forward_kernel(segment, valid, ticket_ref, query_ref, pair_ref, *rest):
    mixed_ref, logsum_ref, value_ref = rest[-3:]
    keys = pair_ref.at[:, PAIR : 2 * PAIR]
    value_ref[:, 0:PAIR] = pair_ref[:, 2 * PAIR : 3 * PAIR]
    value_ref[:, PAIR : 2 * PAIR] = jnp.ones((value_ref.shape[0], PAIR), BF16)
    for chunk in range(query_ref.shape[0] // 128):
        rows = pl.ds(chunk * 128, 128)
        queries = split_pair(query_ref[rows, 0:PAIR])
        scores = mask_keys(dot(queries, keys[...], 1, 1), segment, valid, -1e30)
        peak = jnp.max(scores, axis=1, keepdims=True)
        weights = jnp.exp2((scores - peak) * FACTOR_2).astype(BF16)
        mixed = dot(weights, value_ref[...], 1, 0)
        total = mixed[:, PAIR:]
        mixed_ref[rows, :] = join_pair(mixed[:, :PAIR] / total).astype(BF16)
        logsum_ref[rows, :] = join_pair(peak * FACTOR_2 + jnp.log2(total))


def attend_backward_kernel(
    segment, valid, joint, ticket_ref, query_ref, pair_ref, mixed_ref, grad_ref, logsum_ref, *rest
):
    if joint:
        out_ref, key_sum, value_sum = rest[-3:]
        query_out = out_ref.at[:, 0:PAIR]
        key_out = out_ref.at[:, PAIR : 2 * PAIR]
        value_out = out_ref.at[:, 2 * PAIR : 3 * PAIR]
    else:
        query_out, pair_out, key_sum, value_sum = rest[-4:]
        key_out = pair_out.at[:, 0:PAIR]
        value_out = pair_out.at[:, PAIR : 2 * PAIR]
    keys = pair_ref.at[:, PAIR : 2 * PAIR]
    values = pair_ref.at[:, 2 * PAIR : 3 * PAIR]
    key_total = value_total = None
    for chunk in range(query_ref.shape[0] // 128):
        rows = pl.ds(chunk * 128, 128)
        queries = split_pair(query_ref[rows, 0:PAIR])
        grad = grad_ref[rows, :]
        grads = split_pair(grad)
        row_term = jnp.sum(
            split_pair(grad.astype(F32) * mixed_ref[rows, :].astype(F32)), axis=1, keepdims=True
        )
        logsum = logsum_ref[rows, :]
        logsum = jnp.concatenate([logsum[:, 0:1], logsum[:, HD : HD + 1]], axis=0)
        scores = dot(queries, keys[...], 1, 1)
        probs = mask_keys(jnp.exp2(scores * FACTOR_2 - logsum), segment, valid, 0.0)
        prob_grad = dot(grads, values[...], 1, 1)
        score_grad = (probs * (prob_grad - row_term)).astype(BF16)
        query_grad = join_pair(dot(score_grad, keys[...], 1, 0)) * FACTOR
        query_out[rows, :] = query_grad.astype(BF16)
        value_part = dot(grads.T, probs.astype(BF16), 1, 0)
        key_part = dot(queries.T, score_grad, 1, 0)
        if chunk == 0:
            value_sum[...] = value_part
            key_sum[...] = key_part
        else:
            value_sum[...] += value_part
            key_sum[...] += key_part
    key_out[...] = (key_sum[...] * FACTOR).T.astype(BF16)
    value_out[...] = value_sum[...].T.astype(BF16)


def attend_cost(products, images, pairs, rows, key_rows):
    area = images * pairs * 2 * rows * key_rows
    return pl.CostEstimate(
        flops=2 * products * area * HD * 4,
        bytes_accessed=images * pairs * rows * PAIR * 16,
        transcendentals=area,
    )


def attend_forward(piece, ticket, triple, gathered, kept, segment, valid):
    groups, part_pairs, all_pairs, part_at, all_at = piece
    images, rows, _ = triple.shape
    key_rows = gathered.shape[1]
    pairs = groups * all_pairs
    narrow = lambda i, g, t: (i, 0, g * part_pairs + part_at)
    wide = lambda i, g, t: (i, 0, g * all_pairs + all_at)
    unread = pl.BlockSpec(memory_space=pl.ANY)
    return pl.pallas_call(
        functools.partial(attend_forward_kernel, segment, valid),
        grid_spec=pltpu.PrefetchScalarGridSpec(
            num_scalar_prefetch=1,
            grid=(images, groups),
            in_specs=[
                pl.BlockSpec((None, rows, 3 * PAIR), narrow),
                pl.BlockSpec((None, key_rows, 3 * PAIR), narrow),
            ]
            + [unread] * len(kept),
            out_specs=[
                pl.BlockSpec((None, rows, PAIR), wide),
                pl.BlockSpec((None, rows, PAIR), wide),
            ],
            scratch_shapes=[pltpu.VMEM((key_rows, 2 * PAIR), BF16)],
        ),
        out_shape=[
            jax.ShapeDtypeStruct((images, rows, pairs * PAIR), BF16),
            jax.ShapeDtypeStruct((images, rows, pairs * PAIR), F32),
        ],
        input_output_aliases={3 + place: place for place in range(len(kept))},
        cost_estimate=attend_cost(2, images, groups, rows, key_rows),
        compiler_params=pltpu.CompilerParams(vmem_limit_bytes=VMEM),
    )(ticket, triple, gathered, *kept)


def attend_backward(piece, ticket, triple, gathered, mixed, mixed_grad, logsum, kept, segment, valid):
    groups, part_pairs, all_pairs, part_at, all_at = piece
    images, rows, width = triple.shape
    key_rows = gathered.shape[1]
    joint = key_rows == rows
    narrow = lambda i, g, t: (i, 0, g * part_pairs + part_at)
    wide = lambda i, g, t: (i, 0, g * all_pairs + all_at)
    wide_spec = pl.BlockSpec((None, rows, PAIR), wide)
    triple_spec = pl.BlockSpec((None, rows, 3 * PAIR), narrow)
    pairs = groups * part_pairs
    if joint:
        out_specs = [triple_spec]
        out_shape = [jax.ShapeDtypeStruct(triple.shape, BF16)]
    else:
        out_specs = [
            pl.BlockSpec((None, rows, PAIR), narrow),
            pl.BlockSpec((None, key_rows, 2 * PAIR), narrow),
        ]
        out_shape = [
            jax.ShapeDtypeStruct((images, rows, pairs * PAIR), BF16),
            jax.ShapeDtypeStruct((images, key_rows, pairs * 2 * PAIR), BF16),
        ]
    return pl.pallas_call(
        functools.partial(attend_backward_kernel, segment, valid, joint),
        grid_spec=pltpu.PrefetchScalarGridSpec(
            num_scalar_prefetch=1,
            grid=(images, groups),
            in_specs=[
                triple_spec,
                pl.BlockSpec((None, key_rows, 3 * PAIR), narrow),
                wide_spec,
                wide_spec,
                wide_spec,
            ]
            + [pl.BlockSpec(memory_space=pl.ANY)] * len(kept),
            out_specs=out_specs,
            scratch_shapes=[pltpu.VMEM((PAIR, key_rows), F32)] * 2,
        ),
        out_shape=out_shape,
        input_output_aliases={6 + place: place for place in range(len(kept))},
        cost_estimate=attend_cost(5, images, groups, rows, key_rows),
        compiler_params=pltpu.CompilerParams(vmem_limit_bytes=VMEM),
    )(ticket, triple, gathered, mixed, mixed_grad, logsum, *kept)


def join_grads(outs, pairs, shares, tensor):
    if len(outs) == 1:
        return outs[0]
    query_grad, pair_grad = outs
    images, rows, _ = query_grad.shape
    groups = [list(range(base, base + shares)) for base in range(0, tensor, shares)]
    pair_grad = lax.psum_scatter(
        pair_grad, "tensor", scatter_dimension=1, axis_index_groups=groups, tiled=True
    )
    return jnp.concatenate(
        [
            query_grad.reshape(images, rows, pairs, PAIR),
            pair_grad.reshape(images, rows, pairs, 2 * PAIR),
        ],
        axis=3,
    ).reshape(images, rows, pairs * 3 * PAIR)


def norm_parts(values):
    centre = jnp.mean(values, axis=-1, keepdims=True)
    centred = values - centre
    spread = jnp.mean(centred * centred, axis=-1, keepdims=True)
    inverse = lax.rsqrt(spread + 1e-06)
    return centred * inverse, inverse


def norm_backward(grad, gain, normed, inverse):
    scaled = grad * gain
    return inverse * (
        scaled
        - jnp.mean(scaled, axis=-1, keepdims=True)
        - normed * jnp.mean(scaled * normed, axis=-1, keepdims=True)
    )


TAIL_RATE = 0.3275911 * 0.5**0.5
TAIL = (0.5307027145, -0.7265760135, 0.7107068705, -0.142248368, 0.127414796)


def gelu_parts(values):
    point = 1.0 / (1.0 + TAIL_RATE * jnp.abs(values))
    total = TAIL[0] * point
    for factor in TAIL[1:]:
        total = (total + factor) * point
    bell = jnp.exp2((-0.5 * 1.4426950408889634) * (values * values))
    tail = total * bell
    below = jnp.where(values < 0.0, tail, 1.0 - tail)
    return values * below, below + (values * 0.3989422804014327) * bell


def feed_kernel(tile, *refs):
    (normed_ref, back_ref, expand_ref, reduce_ref, bias_ref) = refs[:5]
    (out_ref, grad_ref, expand_out, reduce_out, bias_out) = refs[5:10]
    (out_sum, grad_sum, active_ref, gate_ref, stage_ref) = refs[10:]
    rows = normed_ref.shape[0]
    expand = expand_ref[...]
    reduce = reduce_ref[...]
    bias = bias_ref[0:1, :]

    def tiles(first):
        total = None
        for base in range(0, rows, tile):
            here = pl.ds(base, tile)
            active, slope = gelu_parts(dot(normed_ref[here, :], expand, 1, 0) + bias)
            active = active.astype(BF16)
            gate = dot(back_ref[here, :], reduce, 1, 0) * slope
            part = jnp.sum(gate.reshape(tile // 8, 8, gate.shape[1]), axis=0)
            total = part if total is None else total + part
            gate = gate.astype(BF16)
            active_ref[here, :] = active
            gate_ref[here, :] = gate
            out = dot(active, reduce, 1, 1)
            grad = dot(gate, expand, 1, 1)
            if first:
                out_sum[here, :] = out
                grad_sum[here, :] = grad
            else:
                out_sum[here, :] += out
                grad_sum[here, :] += grad
        bias_out[...] = total

    @pl.when(pl.program_id(0) == 0)
    def _():
        tiles(True)

    @pl.when(pl.program_id(0) != 0)
    def _():
        tiles(False)

    reduce_out[...] = dot(active_ref[...], back_ref[...], 0, 0).T.astype(BF16)
    expand_out[...] = dot(gate_ref[...], normed_ref[...], 0, 0).T.astype(BF16)

    @pl.when(pl.program_id(0) == pl.num_programs(0) - 1)
    def _():
        stage_rows = stage_ref.shape[0]

        @pl.loop(0, rows // stage_rows)
        def _(i):
            here = pl.ds(pl.multiple_of(i * stage_rows, stage_rows), stage_rows)
            stage_ref[...] = out_sum[here, :].astype(BF16)
            pltpu.sync_copy(stage_ref, out_ref.at[here, :])
            stage_ref[...] = grad_sum[here, :].astype(BF16)
            pltpu.sync_copy(stage_ref, grad_ref.at[here, :])


def feed_forward(normed, back, expand, reduce, bias):
    rows, width = normed.shape
    hidden = expand.shape[1]
    block = 256
    tile = rows // 4
    whole = pl.BlockSpec(memory_space=pltpu.VMEM)
    left = pl.BlockSpec(memory_space=pl.ANY)
    columns = pl.BlockSpec((width, block), lambda f: (0, f))
    vector = pl.BlockSpec((8, block), lambda f: (0, f))
    bias = jnp.broadcast_to(bias[None], (8, hidden))
    out, grad, expand_grad, reduce_grad, bias_grad = pl.pallas_call(
        functools.partial(feed_kernel, tile),
        grid=(hidden // block,),
        in_specs=[whole, whole, columns, columns, vector],
        out_specs=[left, left, columns, columns, vector],
        out_shape=[
            jax.ShapeDtypeStruct((rows, width), BF16),
            jax.ShapeDtypeStruct((rows, width), BF16),
            jax.ShapeDtypeStruct((width, hidden), BF16),
            jax.ShapeDtypeStruct((width, hidden), BF16),
            jax.ShapeDtypeStruct((8, hidden), F32),
        ],
        scratch_shapes=[
            pltpu.VMEM((rows, width), F32),
            pltpu.VMEM((rows, width), F32),
            pltpu.VMEM((rows, block), BF16),
            pltpu.VMEM((rows, block), BF16),
            pltpu.VMEM((128, width), BF16),
        ],
        cost_estimate=pl.CostEstimate(
            flops=12 * rows * width * hidden,
            bytes_accessed=8 * rows * width + 8 * width * hidden,
            transcendentals=rows * hidden,
        ),
        compiler_params=pltpu.CompilerParams(vmem_limit_bytes=60 * 2**20),
    )(normed, back, expand, reduce, bias)
    return out, grad, expand_grad, reduce_grad, jnp.sum(bias_grad, axis=0)


def body(
    mesh,
    tokens,
    cotangent,
    attention_gain,
    attention_shift,
    triple_weight,
    query_bias,
    value_bias,
    merge_weight,
    merge_bias,
    attention_scale,
    forward_gain,
    forward_shift,
    expand_weight,
    expand_bias,
    reduce_weight,
    reduce_bias,
    forward_scale,
):
    tree = Tree(mesh)
    tables = tree.tables()
    count, width = tokens.shape
    segment_rows = min(count, SEQ)
    images = count // segment_rows
    shares = SEQ // segment_rows
    if images * segment_rows != count or shares * segment_rows != SEQ:
        raise ValueError("token rows")
    padded = -(-segment_rows // 128) * 128
    rows = images * padded

    def pad(values):
        shaped = values.reshape(images, segment_rows, width)
        shaped = jnp.pad(shaped, ((0, 0), (0, padded - segment_rows), (0, 0)))
        return shaped.reshape(rows, width)

    def unpad(values):
        return values.reshape(images, padded, width)[:, :segment_rows].reshape(count, width)

    vectors = [
        attention_gain,
        attention_shift,
        query_bias,
        value_bias,
        merge_bias,
        attention_scale,
        forward_gain,
        forward_shift,
        reduce_bias,
        forward_scale,
    ]
    short = attention_gain.shape[0]
    packed = jnp.concatenate([jnp.stack(vectors), expand_bias.reshape(-1, short)], axis=0)
    spare = ((0, -packed.shape[0] % 8), (0, -short % 128))
    gathered = tree.gather_rows(jnp.pad(packed.astype(F32), spare))
    (
        gain_one,
        shift_one,
        query_shift,
        value_shift,
        merge_shift,
        scale_one,
        gain_two,
        shift_two,
        reduce_shift,
        scale_two,
    ) = [gathered[:, place, :short].reshape(-1) for place in range(len(vectors))]
    expand_shift = gathered[:, len(vectors) : packed.shape[0], :short].reshape(-1)

    shard_rows, _, local = triple_weight.shape
    local_pairs = local // PAIR
    parts = 2 if local_pairs % 2 == 0 else 1
    part_pairs = local_pairs // parts
    part_width = part_pairs * 3 * PAIR
    triple_shard = (
        triple_weight.reshape(shard_rows, 3, local_pairs, PAIR)
        .transpose(0, 2, 1, 3)
        .reshape(shard_rows, 3 * local)
    )
    first = tree.gather(jnp.concatenate([triple_shard, merge_weight], axis=1))
    for _ in range(first.stages + 1):
        first.step()
    feed_chain = tree.gather(
        after(jnp.concatenate([expand_weight, reduce_weight], axis=1), first)
    )
    feed_chain.step()
    *triple_full, merge_full = first.finish(
        tables, [part_width] * parts + [merge_weight.shape[1]]
    )

    inputs = pad(tokens).astype(F32)
    normal_one, inverse_one = norm_parts(inputs)
    normed_one = (normal_one * gain_one + shift_one).astype(BF16)
    pairs = tree.tensor * local_pairs
    bias = jnp.stack(
        [
            query_shift.reshape(tree.tensor, parts, part_pairs, PAIR),
            jnp.zeros((tree.tensor, parts, part_pairs, PAIR), F32),
            value_shift.reshape(tree.tensor, parts, part_pairs, PAIR),
        ],
        axis=3,
    )
    triples, pair_rows = [], []
    for part in range(parts):
        triple = dot(normed_one, triple_full[part], 1, 0) + bias[:, part].reshape(-1)
        triple = triple.astype(BF16).reshape(images, padded, -1)
        triples.append(triple)
        if shares > 1:
            groups = [list(range(base, base + shares)) for base in range(0, tree.tensor, shares)]
            triple = lax.all_gather(
                triple, "tensor", axis=1, axis_index_groups=groups, tiled=True
            )
        pair_rows.append(triple)

    places = [(part, at) for part in range(parts) for at in range(part_pairs)]
    ticket = jnp.zeros((1,), jnp.int32)
    kept = ()
    for number, (part, at) in enumerate(places):
        piece = (tree.tensor, part_pairs, local_pairs, at, part * part_pairs + at)
        passed = ticket
        if number in (1, 2):
            passed = after(ticket, feed_chain)
            feed_chain.step()
        kept = attend_forward(
            piece, passed, triples[part], pair_rows[part], kept, padded, segment_rows
        )
    mixed, logsum = kept
    mixed_rows = mixed.reshape(rows, width)
    branch_one = dot(mixed_rows, merge_full, 1, 1) + after(merge_shift, feed_chain)
    middle = inputs + scale_one * branch_one
    normal_two, inverse_two = norm_parts(middle)
    normed_two = (normal_two * gain_two + shift_two).astype(BF16)
    expand_full, reduce_full = feed_chain.finish(
        tables, [expand_weight.shape[1], reduce_weight.shape[1]]
    )

    upstream = pad(cotangent).astype(F32)
    back_two = (upstream * scale_two).astype(BF16)
    feed_out, normed_two_grad, expand_grad, reduce_grad, expand_bias_grad = feed_forward(
        normed_two, back_two, expand_full, reduce_full, expand_shift
    )
    feed_chain = tree.scatter([expand_grad, reduce_grad], tables)
    normed_two_grad = normed_two_grad.astype(F32)
    branch_two = feed_out.astype(F32) + reduce_shift
    result = unpad((middle + scale_two * branch_two).astype(BF16))
    middle_grad = upstream + norm_backward(normed_two_grad, gain_two, normal_two, inverse_two)
    back_one = (middle_grad * scale_one).astype(BF16)
    feed_chain.step()
    mixed_grad = dot(back_one, merge_full, 1, 0).astype(BF16).reshape(images, padded, width)
    merge_grad = dot(back_one, mixed_rows, 0, 0).astype(BF16)
    chains, part_grads, kept = [feed_chain], [], ()
    for number, (part, at) in enumerate(places):
        piece = (tree.tensor, part_pairs, local_pairs, at, part * part_pairs + at)
        kept = attend_backward(
            piece,
            after(ticket, *chains),
            triples[part],
            pair_rows[part],
            mixed,
            mixed_grad,
            logsum,
            kept,
            padded,
            segment_rows,
        )
        for chain in chains:
            chain.step()
        if at == part_pairs - 1:
            grad = join_grads(kept, tree.tensor * part_pairs, shares, tree.tensor)
            grad = grad.reshape(rows, -1)
            part_grads.append(grad)
            kept = ()
            sent = [dot(normed_one, grad, 0, 0).astype(BF16)]
            if part == 0:
                sent.append(merge_grad)
            chains.append(tree.scatter(sent, tables))
            if part + 1 < parts:
                chains[-1].step()
    normed_one_grad = None
    for grad, full_part in zip(part_grads, triple_full):
        term = dot(grad, after(full_part, *chains[1:]), 1, 1)
        normed_one_grad = term if normed_one_grad is None else normed_one_grad + term
        for chain in chains:
            chain.step()
    late_gain = after(gain_one, *chains[1:])
    tokens_grad = middle_grad + norm_backward(normed_one_grad, late_gain, normal_one, inverse_one)
    tokens_grad = unpad(tokens_grad.astype(BF16))
    expand_out, reduce_out = chains[0].finish()
    first_out, merge_out = chains[1].finish()
    triple_parts = [first_out] + [chain.finish()[0] for chain in chains[2:]]
    triple_out = jnp.concatenate(
        [part.reshape(shard_rows, part_pairs, 3, PAIR) for part in triple_parts], axis=1
    )
    triple_out = triple_out.transpose(0, 2, 1, 3).reshape(shard_rows, 3, local)

    bias_sums = jnp.stack(
        [
            jnp.sum(grad, axis=0, dtype=F32).reshape(tree.tensor, part_pairs, 3, PAIR)
            for grad in part_grads
        ],
        axis=1,
    )
    sums = [
        jnp.sum(normed_one_grad * normal_one, axis=0),
        jnp.sum(normed_one_grad, axis=0),
        bias_sums[:, :, :, 0].reshape(-1),
        bias_sums[:, :, :, 2].reshape(-1),
        jnp.sum(middle_grad, axis=0) * scale_one,
        jnp.sum(middle_grad * branch_one, axis=0),
        jnp.sum(normed_two_grad * normal_two, axis=0),
        jnp.sum(normed_two_grad, axis=0),
        jnp.sum(upstream, axis=0) * scale_two,
        jnp.sum(upstream * branch_two, axis=0),
        expand_bias_grad,
    ]
    columns = jnp.concatenate(
        [total.reshape(tree.dp, -1, short) for total in sums[:-1]]
        + [sums[-1].reshape(tree.dp, -1, short)],
        axis=1,
    )
    mine = tree.scatter_rows(jnp.pad(columns, ((0, 0),) + spare))
    vector_out = [mine[place, :short] for place in range(len(vectors))]
    vector_out.append(mine[len(vectors) : packed.shape[0], :short].reshape(-1))
    return (
        result,
        tokens_grad,
        vector_out[0],
        vector_out[1],
        triple_out,
        vector_out[2],
        vector_out[3],
        merge_out,
        vector_out[4],
        vector_out[5],
        vector_out[6],
        vector_out[7],
        expand_out,
        vector_out[10],
        reduce_out,
        vector_out[8],
        vector_out[9],
    )


def solution(mesh):
    rows = P(("dp", "tensor"), None)
    vector = P("dp")
    weight = P("dp", "tensor")
    triple = P("dp", None, "tensor")
    parameters = (
        vector,
        vector,
        triple,
        vector,
        vector,
        weight,
        vector,
        vector,
        vector,
        vector,
        weight,
        vector,
        weight,
        vector,
        vector,
    )
    return jax.shard_map(
        functools.partial(body, mesh),
        mesh=mesh,
        in_specs=(rows, rows) + parameters,
        out_specs=(rows, rows) + parameters,
        check_vma=False,
    )
```

```python
import functools

import jax
import jax.numpy as jnp
from jax import lax
from jax.experimental import pallas as pl
from jax.experimental.pallas import tpu as pltpu
from jax.sharding import PartitionSpec as P

HD = 64
SEQ = 1370
PAIR = 128
F32 = jnp.float32
BF16 = jnp.bfloat16
FACTOR = HD ** (-0.5)
FACTOR_2 = FACTOR * 1.4426950408889634
VMEM = 56 * 2**20


def dot(left, right, left_dim, right_dim):
    dims = (((left_dim,), (right_dim,)), ((), ()))
    return lax.dot_general(left, right, dims, preferred_element_type=F32)


class Tree:
    def __init__(self, mesh):
        self.dp = mesh.shape["dp"]
        self.tensor = mesh.shape["tensor"]
        dp_bits = self.dp.bit_length() - 1
        tensor_bits = self.tensor.bit_length() - 1
        if 1 << dp_bits != self.dp or 1 << tensor_bits != self.tensor or dp_bits < 2:
            raise ValueError("mesh sizes")
        high = [("dp", tuple(range(dp_bits - 1, 1, -1)))]
        tensor_stages = [("tensor", (bit,)) for bit in range(tensor_bits - 1, -1, -1)]
        self.orders = (
            high + [("dp", (1,))] + tensor_stages,
            high + tensor_stages + [("dp", (1,))],
        )
        self.half_blocks = self.dp * self.tensor // 2

    def masks(self, stage):
        bits = stage[1]
        return [
            sum(1 << bit for place, bit in enumerate(bits) if choice >> place & 1)
            for choice in range(1, 1 << len(bits))
        ]

    def swap(self, value, axis, mask):
        size = self.dp if axis == "dp" else self.tensor
        return lax.ppermute(value, axis, [(i, i ^ mask) for i in range(size)])

    def spread(self, held, stage):
        return jnp.concatenate(
            [held] + [self.swap(held, stage[0], mask) for mask in self.masks(stage)], axis=0
        )

    def add_up(self, held, stage):
        size = held.shape[0] >> len(stage[1])
        total = held[:size]
        for place, mask in enumerate(self.masks(stage), 1):
            total = total + self.swap(held[place * size : (place + 1) * size], stage[0], mask)
        return total

    def tables(self):
        me_dp = lax.axis_index("dp")
        me_tensor = lax.axis_index("tensor")
        place = jnp.arange(self.half_blocks, dtype=jnp.int32)
        pairs = self.dp // 2
        relative = {
            "dp": ((place % pairs) << 1) ^ (me_dp & ~1),
            "tensor": (place // pairs) ^ me_tensor,
        }
        rows = []
        for order in self.orders:
            index = jnp.zeros_like(place)
            flat = [(axis, bit) for axis, bits in order for bit in bits]
            for position, (axis, bit) in enumerate(flat):
                index = index + (((relative[axis] >> bit) & 1) << position)
            rows.append(index)
        core = jnp.full_like(place, me_dp & 1)
        return jnp.stack(rows + [core]).astype(jnp.int32)

    def gather(self, shard):
        return Gather(self, [shard[None]])

    def assemble(self, pieces, tables, half, widths):
        pairs = self.dp // 2
        total = sum(widths)
        if 4 * half * self.half_blocks * total < 5 * 2**20:
            return self.assemble_whole(pieces, tables, half, widths)

        def kernel(tables_ref, own_a, far_a, own_b, far_b, *outs):
            core = tables_ref[2, 0]

            def put(first_a, second_a, first_b, second_b):
                at = 0
                for out, width in zip(outs, widths):
                    columns = slice(at, at + width)
                    out[0:half] = first_a[:, columns]
                    out[half : 2 * half] = first_b[:, columns]
                    out[2 * half : 3 * half] = second_a[:, columns]
                    out[3 * half : 4 * half] = second_b[:, columns]
                    at += width

            @pl.when(core == 0)
            def _():
                put(own_a, far_a, own_b, far_b)

            @pl.when(core != 0)
            def _():
                put(far_a, own_a, far_b, own_b)

        spec_a = pl.BlockSpec((None, half, total), lambda i, table: (table[0, i], 0, 0))
        spec_b = pl.BlockSpec((None, half, total), lambda i, table: (table[1, i], 0, 0))
        return pl.pallas_call(
            kernel,
            grid_spec=pltpu.PrefetchScalarGridSpec(
                num_scalar_prefetch=1,
                grid=(self.half_blocks,),
                in_specs=[spec_a, spec_a, spec_b, spec_b],
                out_specs=[
                    pl.BlockSpec((4 * half, width), lambda i, table: (i % pairs, i // pairs))
                    for width in widths
                ],
            ),
            out_shape=[
                jax.ShapeDtypeStruct((self.dp * 2 * half, self.tensor * width), BF16)
                for width in widths
            ],
            compiler_params=pltpu.CompilerParams(vmem_limit_bytes=VMEM),
        )(tables, *pieces)

    def assemble_whole(self, pieces, tables, half, widths):
        pairs = self.dp // 2

        def kernel(tables_ref, own_a, far_a, own_b, far_b, *outs):
            core = tables_ref[2, 0]

            @pl.loop(0, pairs)
            def _(pair):
                own = pl.multiple_of((2 * pair + core) * 2 * half, 2 * half)
                far = pl.multiple_of((2 * pair + 1 - core) * 2 * half, 2 * half)
                for tensor in range(self.tensor):
                    at_a = tables_ref[0, tensor * pairs + pair]
                    at_b = tables_ref[1, tensor * pairs + pair]
                    at = 0
                    for out, width in zip(outs, widths):
                        source = slice(at, at + width)
                        columns = slice(tensor * width, (tensor + 1) * width)
                        out[pl.ds(own, half), columns] = own_a[at_a, :, source]
                        out[pl.ds(own + half, half), columns] = own_b[at_b, :, source]
                        out[pl.ds(far, half), columns] = far_a[at_a, :, source]
                        out[pl.ds(far + half, half), columns] = far_b[at_b, :, source]
                        at += width

        return self.whole_call(
            kernel,
            tables,
            pieces,
            [(self.dp * 2 * half, self.tensor * width) for width in widths],
        )

    def split_whole(self, arrays, tables, half, widths):
        pairs = self.dp // 2

        def kernel(tables_ref, *refs):
            sources, (own_a, far_a, own_b, far_b) = refs[: len(widths)], refs[len(widths) :]
            core = tables_ref[2, 0]

            @pl.loop(0, pairs)
            def _(pair):
                own = pl.multiple_of((2 * pair + core) * 2 * half, 2 * half)
                far = pl.multiple_of((2 * pair + 1 - core) * 2 * half, 2 * half)
                for tensor in range(self.tensor):
                    at_a = tables_ref[0, tensor * pairs + pair]
                    at_b = tables_ref[1, tensor * pairs + pair]
                    at = 0
                    for source, width in zip(sources, widths):
                        target = slice(at, at + width)
                        columns = slice(tensor * width, (tensor + 1) * width)
                        own_a[at_a, :, target] = source[pl.ds(own, half), columns]
                        own_b[at_b, :, target] = source[pl.ds(own + half, half), columns]
                        far_a[at_a, :, target] = source[pl.ds(far, half), columns]
                        far_b[at_b, :, target] = source[pl.ds(far + half, half), columns]
                        at += width

        return self.whole_call(
            kernel, tables, arrays, [(self.half_blocks, half, sum(widths))] * 4
        )

    def whole_call(self, kernel, tables, values, shapes):
        vmem = pl.BlockSpec(memory_space=pltpu.VMEM)
        return pl.pallas_call(
            kernel,
            in_specs=[pl.BlockSpec(memory_space=pltpu.SMEM)] + [vmem] * len(values),
            out_specs=[vmem] * len(shapes),
            out_shape=[jax.ShapeDtypeStruct(shape, BF16) for shape in shapes],
            compiler_params=pltpu.CompilerParams(vmem_limit_bytes=VMEM),
        )(tables, *values)

    def split(self, arrays, tables, half, widths):
        pairs = self.dp // 2
        total = sum(widths)
        if 4 * half * self.half_blocks * total < 5 * 2**20:
            return self.split_whole(arrays, tables, half, widths)

        def kernel(tables_ref, *refs):
            sources, (own_a, far_a, own_b, far_b) = refs[: len(widths)], refs[len(widths) :]
            core = tables_ref[2, 0]

            def take(first_a, second_a, first_b, second_b):
                at = 0
                for source, width in zip(sources, widths):
                    columns = slice(at, at + width)
                    first_a[:, columns] = source[0:half]
                    first_b[:, columns] = source[half : 2 * half]
                    second_a[:, columns] = source[2 * half : 3 * half]
                    second_b[:, columns] = source[3 * half : 4 * half]
                    at += width

            @pl.when(core == 0)
            def _():
                take(own_a, far_a, own_b, far_b)

            @pl.when(core != 0)
            def _():
                take(far_a, own_a, far_b, own_b)

        spec_a = pl.BlockSpec((None, half, total), lambda i, table: (table[0, i], 0, 0))
        spec_b = pl.BlockSpec((None, half, total), lambda i, table: (table[1, i], 0, 0))
        shape = jax.ShapeDtypeStruct((self.half_blocks, half, total), BF16)
        return pl.pallas_call(
            kernel,
            grid_spec=pltpu.PrefetchScalarGridSpec(
                num_scalar_prefetch=1,
                grid=(self.half_blocks,),
                in_specs=[
                    pl.BlockSpec((4 * half, width), lambda i, table: (i % pairs, i // pairs))
                    for width in widths
                ],
                out_specs=[spec_a, spec_a, spec_b, spec_b],
            ),
            out_shape=[shape] * 4,
            compiler_params=pltpu.CompilerParams(vmem_limit_bytes=VMEM),
        )(tables, *arrays)

    def scatter(self, arrays, tables):
        rows = arrays[0].shape[0] // self.dp
        widths = [array.shape[1] // self.tensor for array in arrays]
        return Scatter(self, self.split(arrays, tables, rows // 2, widths), widths)

    def row_stages(self):
        bits = tuple(range(self.dp.bit_length() - 1))
        return [("dp", bits[2:]), ("dp", bits[:2])]

    def gather_rows(self, row):
        held = row[None]
        stages = self.row_stages()
        for stage in stages:
            held = self.spread(held, stage)
        relative = jnp.arange(self.dp) ^ lax.axis_index("dp")
        index = jnp.zeros_like(relative)
        for position, bit in enumerate(bit for stage in stages for bit in stage[1]):
            index = index + (((relative >> bit) & 1) << position)
        return held[index]

    def scatter_rows(self, rows):
        stages = self.row_stages()
        place = jnp.arange(self.dp)
        relative = jnp.zeros_like(place)
        for position, bit in enumerate(bit for stage in stages for bit in stage[1]):
            relative = relative + (((place >> position) & 1) << bit)
        held = rows[relative ^ lax.axis_index("dp")]
        for bit in range(self.tensor.bit_length() - 1):
            held = held + self.swap(held, "tensor", 1 << bit)
        for stage in stages[::-1]:
            held = self.add_up(held, stage)
        return held[0]


class Gather:
    def __init__(self, tree, held):
        self.tree = tree
        self.held = held
        self.done = 0
        self.stages = len(tree.orders[0])

    def step(self):
        if self.done == 0:
            whole = self.tree.spread(self.held[0], self.tree.orders[0][0])
            half = whole.shape[1] // 2
            self.held = [whole[:, :half], whole[:, half:]]
        elif self.done < self.stages:
            self.held = [
                self.tree.spread(held, order[self.done])
                for held, order in zip(self.held, self.tree.orders)
            ]
        elif self.done == self.stages:
            self.held = self.held + [self.tree.swap(held, "dp", 1) for held in self.held]
        self.done += 1

    def finish(self, tables, widths):
        while self.done <= self.stages:
            self.step()
        own_a, own_b, far_a, far_b = self.held
        half = own_a.shape[1]
        return self.tree.assemble([own_a, far_a, own_b, far_b], tables, half, widths)


class Scatter:
    def __init__(self, tree, pieces, widths):
        own_a, far_a, own_b, far_b = pieces
        self.tree = tree
        self.widths = widths
        self.held = [own_a, own_b]
        self.sent = [[far_a], [far_b]]
        self.orders = [[("dp", (0,))] + order[::-1] for order in tree.orders]
        self.done = 0

    def step(self):
        if self.issued():
            return
        totals = []
        for held, sent, order in zip(self.held, self.sent, self.orders):
            axis = order[self.done][0]
            total = held.astype(F32)
            for value, mask in zip(sent, self.tree.masks(order[self.done])):
                total = total + self.tree.swap(value, axis, mask).astype(F32)
            totals.append(total)
        self.done += 1
        if self.issued():
            self.held, self.sent = totals, []
            return
        if self.done + 1 == len(self.orders[0]):
            totals = [jnp.concatenate(totals, axis=1)]
        self.held, self.sent = [], []
        for total, order in zip(totals, self.orders):
            total = total.astype(BF16)
            count = 1 << len(order[self.done][1])
            size = total.shape[0] // count
            parts = [total[place * size : (place + 1) * size] for place in range(count)]
            self.held.append(parts[0])
            self.sent.append(parts[1:])

    def issued(self):
        return self.done == len(self.orders[0])

    def finish(self):
        while not self.issued():
            self.step()
        whole = self.held[0][0]
        parts, at = [], 0
        for width in self.widths:
            parts.append(whole[:, at : at + width])
            at += width
        return parts


def held_by(*chains):
    arrays = []
    for chain in chains:
        arrays += chain.held
        for sent in getattr(chain, "sent", ()):
            arrays += sent
    return arrays


def hold(arrays, *others):
    count = len(arrays)

    def kernel(*refs):
        refs[-1][...] = jnp.zeros(refs[-1].shape, F32)

    unread = pl.BlockSpec(memory_space=pl.ANY)
    outs = pl.pallas_call(
        kernel,
        in_specs=[unread] * (count + len(others)),
        out_specs=[unread] * count + [pl.BlockSpec(memory_space=pltpu.VMEM)],
        out_shape=[jax.ShapeDtypeStruct(array.shape, array.dtype) for array in arrays]
        + [jax.ShapeDtypeStruct((8, 128), F32)],
        input_output_aliases={place: place for place in range(count)},
    )(*arrays, *others)
    return list(outs[:count])


def after(value, *arrays):
    for array in arrays:
        value = value + (array[(0,) * array.ndim].astype(F32) * 0.0).astype(value.dtype)
    return value


def split_pair(block):
    lane = lax.broadcasted_iota(jnp.int32, block.shape, 1)
    zero = jnp.zeros_like(block)
    return jnp.concatenate(
        [jnp.where(lane < HD, block, zero), jnp.where(lane >= HD, block, zero)], axis=0
    )


def join_pair(block):
    rows = block.shape[0] // 2
    lane = lax.broadcasted_iota(jnp.int32, (rows, PAIR), 1)
    return jnp.where(lane < HD, block[:rows], block[rows:])


def mask_keys(scores, segment, valid, fill):
    if valid == segment:
        return scores
    start = valid // 128 * 128
    parts = []
    for base in range(0, scores.shape[1], segment):
        if start:
            parts.append(scores[:, base : base + start])
        tail = scores[:, base + start : base + segment]
        lane = lax.broadcasted_iota(jnp.int32, tail.shape, 1) + start
        parts.append(jnp.where(lane < valid, tail, fill))
    return jnp.concatenate(parts, axis=1)


def attend_forward_kernel(segment, valid, ticket_ref, query_ref, pair_ref, *rest):
    mixed_ref, logsum_ref, value_ref = rest[-3:]
    keys = pair_ref.at[:, PAIR : 2 * PAIR]
    value_ref[:, 0:PAIR] = pair_ref[:, 2 * PAIR : 3 * PAIR]
    value_ref[:, PAIR : 2 * PAIR] = jnp.ones((value_ref.shape[0], PAIR), BF16)
    for chunk in range(query_ref.shape[0] // 128):
        rows = pl.ds(chunk * 128, 128)
        queries = split_pair(query_ref[rows, 0:PAIR])
        scores = mask_keys(dot(queries, keys[...], 1, 1), segment, valid, -1e30)
        peak = jnp.max(scores, axis=1, keepdims=True)
        weights = jnp.exp2((scores - peak) * FACTOR_2).astype(BF16)
        mixed = dot(weights, value_ref[...], 1, 0)
        total = mixed[:, PAIR:]
        mixed_ref[rows, :] = join_pair(mixed[:, :PAIR] / total).astype(BF16)
        logsum_ref[rows, :] = join_pair(peak * FACTOR_2 + jnp.log2(total))


def attend_backward_kernel(
    segment, valid, joint, ticket_ref, query_ref, pair_ref, mixed_ref, grad_ref, logsum_ref, *rest
):
    if joint:
        out_ref, key_sum, value_sum = rest[-3:]
        query_out = out_ref.at[:, 0:PAIR]
        key_out = out_ref.at[:, PAIR : 2 * PAIR]
        value_out = out_ref.at[:, 2 * PAIR : 3 * PAIR]
    else:
        query_out, pair_out, key_sum, value_sum = rest[-4:]
        key_out = pair_out.at[:, 0:PAIR]
        value_out = pair_out.at[:, PAIR : 2 * PAIR]
    keys = pair_ref.at[:, PAIR : 2 * PAIR]
    values = pair_ref.at[:, 2 * PAIR : 3 * PAIR]
    key_total = value_total = None
    for chunk in range(query_ref.shape[0] // 128):
        rows = pl.ds(chunk * 128, 128)
        queries = split_pair(query_ref[rows, 0:PAIR])
        grad = grad_ref[rows, :]
        grads = split_pair(grad)
        row_term = jnp.sum(
            split_pair(grad.astype(F32) * mixed_ref[rows, :].astype(F32)), axis=1, keepdims=True
        )
        logsum = logsum_ref[rows, :]
        logsum = jnp.concatenate([logsum[:, 0:1], logsum[:, HD : HD + 1]], axis=0)
        scores = dot(queries, keys[...], 1, 1)
        probs = mask_keys(jnp.exp2(scores * FACTOR_2 - logsum), segment, valid, 0.0)
        prob_grad = dot(grads, values[...], 1, 1)
        score_grad = (probs * (prob_grad - row_term)).astype(BF16)
        query_grad = join_pair(dot(score_grad, keys[...], 1, 0)) * FACTOR
        query_out[rows, :] = query_grad.astype(BF16)
        value_part = dot(grads.T, probs.astype(BF16), 1, 0)
        key_part = dot(queries.T, score_grad, 1, 0)
        if chunk == 0:
            value_sum[...] = value_part
            key_sum[...] = key_part
        else:
            value_sum[...] += value_part
            key_sum[...] += key_part
    key_out[...] = (key_sum[...] * FACTOR).T.astype(BF16)
    value_out[...] = value_sum[...].T.astype(BF16)


def attend_cost(products, images, pairs, rows, key_rows):
    area = images * pairs * 2 * rows * key_rows
    return pl.CostEstimate(
        flops=2 * products * area * HD * 4,
        bytes_accessed=images * pairs * rows * PAIR * 16,
        transcendentals=area,
    )


def attend_forward(piece, ticket, triple, gathered, kept, waits, segment, valid):
    groups, part_pairs, all_pairs, part_at, all_at = piece
    images, rows, _ = triple.shape
    key_rows = gathered.shape[1]
    pairs = groups * all_pairs
    narrow = lambda i, g, t: (i, 0, g * part_pairs + part_at)
    wide = lambda i, g, t: (i, 0, g * all_pairs + all_at)
    unread = pl.BlockSpec(memory_space=pl.ANY)
    return pl.pallas_call(
        functools.partial(attend_forward_kernel, segment, valid),
        grid_spec=pltpu.PrefetchScalarGridSpec(
            num_scalar_prefetch=1,
            grid=(images, groups),
            in_specs=[
                pl.BlockSpec((None, rows, 3 * PAIR), narrow),
                pl.BlockSpec((None, key_rows, 3 * PAIR), narrow),
            ]
            + [unread] * (len(kept) + len(waits)),
            out_specs=[
                pl.BlockSpec((None, rows, PAIR), wide),
                pl.BlockSpec((None, rows, PAIR), wide),
            ],
            scratch_shapes=[pltpu.VMEM((key_rows, 2 * PAIR), BF16)],
        ),
        out_shape=[
            jax.ShapeDtypeStruct((images, rows, pairs * PAIR), BF16),
            jax.ShapeDtypeStruct((images, rows, pairs * PAIR), F32),
        ],
        input_output_aliases={3 + place: place for place in range(len(kept))},
        cost_estimate=attend_cost(2, images, groups, rows, key_rows),
        compiler_params=pltpu.CompilerParams(vmem_limit_bytes=VMEM),
    )(ticket, triple, gathered, *kept, *waits)


def attend_backward(
    piece, ticket, triple, gathered, mixed, mixed_grad, logsum, kept, waits, segment, valid
):
    groups, part_pairs, all_pairs, part_at, all_at = piece
    images, rows, width = triple.shape
    key_rows = gathered.shape[1]
    joint = key_rows == rows
    narrow = lambda i, g, t: (i, 0, g * part_pairs + part_at)
    wide = lambda i, g, t: (i, 0, g * all_pairs + all_at)
    wide_spec = pl.BlockSpec((None, rows, PAIR), wide)
    triple_spec = pl.BlockSpec((None, rows, 3 * PAIR), narrow)
    pairs = groups * part_pairs
    if joint:
        out_specs = [triple_spec]
        out_shape = [jax.ShapeDtypeStruct(triple.shape, BF16)]
    else:
        out_specs = [
            pl.BlockSpec((None, rows, PAIR), narrow),
            pl.BlockSpec((None, key_rows, 2 * PAIR), narrow),
        ]
        out_shape = [
            jax.ShapeDtypeStruct((images, rows, pairs * PAIR), BF16),
            jax.ShapeDtypeStruct((images, key_rows, pairs * 2 * PAIR), BF16),
        ]
    return pl.pallas_call(
        functools.partial(attend_backward_kernel, segment, valid, joint),
        grid_spec=pltpu.PrefetchScalarGridSpec(
            num_scalar_prefetch=1,
            grid=(images, groups),
            in_specs=[
                triple_spec,
                pl.BlockSpec((None, key_rows, 3 * PAIR), narrow),
                wide_spec,
                wide_spec,
                wide_spec,
            ]
            + [pl.BlockSpec(memory_space=pl.ANY)] * (len(kept) + len(waits)),
            out_specs=out_specs,
            scratch_shapes=[pltpu.VMEM((PAIR, key_rows), F32)] * 2,
        ),
        out_shape=out_shape,
        input_output_aliases={6 + place: place for place in range(len(kept))},
        cost_estimate=attend_cost(5, images, groups, rows, key_rows),
        compiler_params=pltpu.CompilerParams(vmem_limit_bytes=VMEM),
    )(ticket, triple, gathered, mixed, mixed_grad, logsum, *kept, *waits)


def join_grads(outs, pairs, shares, tensor):
    if len(outs) == 1:
        return outs[0]
    query_grad, pair_grad = outs
    images, rows, _ = query_grad.shape
    groups = [list(range(base, base + shares)) for base in range(0, tensor, shares)]
    pair_grad = lax.psum_scatter(
        pair_grad, "tensor", scatter_dimension=1, axis_index_groups=groups, tiled=True
    )
    return jnp.concatenate(
        [
            query_grad.reshape(images, rows, pairs, PAIR),
            pair_grad.reshape(images, rows, pairs, 2 * PAIR),
        ],
        axis=3,
    ).reshape(images, rows, pairs * 3 * PAIR)


def norm_parts(values):
    centre = jnp.mean(values, axis=-1, keepdims=True)
    centred = values - centre
    spread = jnp.mean(centred * centred, axis=-1, keepdims=True)
    inverse = lax.rsqrt(spread + 1e-06)
    return centred * inverse, inverse


def norm_backward(grad, gain, normed, inverse):
    scaled = grad * gain
    return inverse * (
        scaled
        - jnp.mean(scaled, axis=-1, keepdims=True)
        - normed * jnp.mean(scaled * normed, axis=-1, keepdims=True)
    )


TAIL_RATE = 0.3275911 * 0.5**0.5
TAIL = (0.5307027145, -0.7265760135, 0.7107068705, -0.142248368, 0.127414796)


def gelu_parts(values):
    point = 1.0 / (1.0 + TAIL_RATE * jnp.abs(values))
    total = TAIL[0] * point
    for factor in TAIL[1:]:
        total = (total + factor) * point
    bell = jnp.exp2((-0.5 * 1.4426950408889634) * (values * values))
    tail = total * bell
    below = jnp.where(values < 0.0, tail, 1.0 - tail)
    return values * below, below + (values * 0.3989422804014327) * bell


def feed_kernel(tile, *refs):
    (normed_ref, back_ref, expand_ref, reduce_ref, bias_ref) = refs[:5]
    (out_ref, grad_ref, expand_out, reduce_out, bias_out) = refs[5:10]
    (out_sum, grad_sum, active_ref, gate_ref, stage_ref) = refs[10:]
    rows = normed_ref.shape[0]
    expand = expand_ref[...]
    reduce = reduce_ref[...]
    bias = bias_ref[0:1, :]

    def tiles(first):
        total = None
        for base in range(0, rows, tile):
            here = pl.ds(base, tile)
            active, slope = gelu_parts(dot(normed_ref[here, :], expand, 1, 0) + bias)
            active = active.astype(BF16)
            gate = dot(back_ref[here, :], reduce, 1, 0) * slope
            part = jnp.sum(gate.reshape(tile // 8, 8, gate.shape[1]), axis=0)
            total = part if total is None else total + part
            gate = gate.astype(BF16)
            active_ref[here, :] = active
            gate_ref[here, :] = gate
            out = dot(active, reduce, 1, 1)
            grad = dot(gate, expand, 1, 1)
            if first:
                out_sum[here, :] = out
                grad_sum[here, :] = grad
            else:
                out_sum[here, :] += out
                grad_sum[here, :] += grad
        bias_out[...] = total

    @pl.when(pl.program_id(0) == 0)
    def _():
        tiles(True)

    @pl.when(pl.program_id(0) != 0)
    def _():
        tiles(False)

    reduce_out[...] = dot(active_ref[...], back_ref[...], 0, 0).T.astype(BF16)
    expand_out[...] = dot(gate_ref[...], normed_ref[...], 0, 0).T.astype(BF16)

    @pl.when(pl.program_id(0) == pl.num_programs(0) - 1)
    def _():
        stage_rows = stage_ref.shape[0]

        @pl.loop(0, rows // stage_rows)
        def _(i):
            here = pl.ds(pl.multiple_of(i * stage_rows, stage_rows), stage_rows)
            stage_ref[...] = out_sum[here, :].astype(BF16)
            pltpu.sync_copy(stage_ref, out_ref.at[here, :])
            stage_ref[...] = grad_sum[here, :].astype(BF16)
            pltpu.sync_copy(stage_ref, grad_ref.at[here, :])


def feed_forward(normed, back, expand, reduce, bias):
    rows, width = normed.shape
    hidden = expand.shape[1]
    block = 256
    tile = rows // 4
    whole = pl.BlockSpec(memory_space=pltpu.VMEM)
    left = pl.BlockSpec(memory_space=pl.ANY)
    columns = pl.BlockSpec((width, block), lambda f: (0, f))
    vector = pl.BlockSpec((8, block), lambda f: (0, f))
    bias = jnp.broadcast_to(bias[None], (8, hidden))
    out, grad, expand_grad, reduce_grad, bias_grad = pl.pallas_call(
        functools.partial(feed_kernel, tile),
        grid=(hidden // block,),
        in_specs=[whole, whole, columns, columns, vector],
        out_specs=[left, left, columns, columns, vector],
        out_shape=[
            jax.ShapeDtypeStruct((rows, width), BF16),
            jax.ShapeDtypeStruct((rows, width), BF16),
            jax.ShapeDtypeStruct((width, hidden), BF16),
            jax.ShapeDtypeStruct((width, hidden), BF16),
            jax.ShapeDtypeStruct((8, hidden), F32),
        ],
        scratch_shapes=[
            pltpu.VMEM((rows, width), F32),
            pltpu.VMEM((rows, width), F32),
            pltpu.VMEM((rows, block), BF16),
            pltpu.VMEM((rows, block), BF16),
            pltpu.VMEM((128, width), BF16),
        ],
        cost_estimate=pl.CostEstimate(
            flops=12 * rows * width * hidden,
            bytes_accessed=8 * rows * width + 8 * width * hidden,
            transcendentals=rows * hidden,
        ),
        compiler_params=pltpu.CompilerParams(vmem_limit_bytes=60 * 2**20),
    )(normed, back, expand, reduce, bias)
    return out, grad, expand_grad, reduce_grad, jnp.sum(bias_grad, axis=0)


def body(
    mesh,
    tokens,
    cotangent,
    attention_gain,
    attention_shift,
    triple_weight,
    query_bias,
    value_bias,
    merge_weight,
    merge_bias,
    attention_scale,
    forward_gain,
    forward_shift,
    expand_weight,
    expand_bias,
    reduce_weight,
    reduce_bias,
    forward_scale,
):
    tree = Tree(mesh)
    tables = tree.tables()
    count, width = tokens.shape
    segment_rows = min(count, SEQ)
    images = count // segment_rows
    shares = SEQ // segment_rows
    if images * segment_rows != count or shares * segment_rows != SEQ:
        raise ValueError("token rows")
    padded = -(-segment_rows // 128) * 128
    rows = images * padded

    def pad(values):
        shaped = values.reshape(images, segment_rows, width)
        shaped = jnp.pad(shaped, ((0, 0), (0, padded - segment_rows), (0, 0)))
        return shaped.reshape(rows, width)

    def unpad(values):
        return values.reshape(images, padded, width)[:, :segment_rows].reshape(count, width)

    vectors = [
        attention_gain,
        attention_shift,
        query_bias,
        value_bias,
        merge_bias,
        attention_scale,
        forward_gain,
        forward_shift,
        reduce_bias,
        forward_scale,
    ]
    short = attention_gain.shape[0]
    packed = jnp.concatenate([jnp.stack(vectors), expand_bias.reshape(-1, short)], axis=0)
    spare = ((0, -packed.shape[0] % 8), (0, -short % 128))
    gathered = tree.gather_rows(jnp.pad(packed.astype(F32), spare))
    (
        gain_one,
        shift_one,
        query_shift,
        value_shift,
        merge_shift,
        scale_one,
        gain_two,
        shift_two,
        reduce_shift,
        scale_two,
    ) = [gathered[:, place, :short].reshape(-1) for place in range(len(vectors))]
    expand_shift = gathered[:, len(vectors) : packed.shape[0], :short].reshape(-1)

    shard_rows, _, local = triple_weight.shape
    local_pairs = local // PAIR
    parts = 2 if local_pairs % 2 == 0 else 1
    part_pairs = local_pairs // parts
    part_width = part_pairs * 3 * PAIR
    triple_shard = (
        triple_weight.reshape(shard_rows, 3, local_pairs, PAIR)
        .transpose(0, 2, 1, 3)
        .reshape(shard_rows, 3 * local)
    )
    inputs = pad(tokens).astype(F32)
    normal_one, inverse_one = norm_parts(inputs)
    normed_one = (normal_one * gain_one + shift_one).astype(BF16)
    first = tree.gather(jnp.concatenate([triple_shard, merge_weight], axis=1))
    first.step()
    feed_chain = tree.gather(
        after(jnp.concatenate([expand_weight, reduce_weight], axis=1), *first.held)
    )
    feed_chain.step()
    first.step()
    while first.done < first.stages:
        first.step()
    first.step()
    *triple_full, merge_full = first.finish(
        tables, [part_width] * parts + [merge_weight.shape[1]]
    )
    pairs = tree.tensor * local_pairs
    bias = jnp.stack(
        [
            query_shift.reshape(tree.tensor, parts, part_pairs, PAIR),
            jnp.zeros((tree.tensor, parts, part_pairs, PAIR), F32),
            value_shift.reshape(tree.tensor, parts, part_pairs, PAIR),
        ],
        axis=3,
    )
    triples, pair_rows = [], []
    for part in range(parts):
        triple = dot(normed_one, triple_full[part], 1, 0) + bias[:, part].reshape(-1)
        triple = triple.astype(BF16).reshape(images, padded, -1)
        triples.append(triple)
        if shares > 1:
            groups = [list(range(base, base + shares)) for base in range(0, tree.tensor, shares)]
            triple = lax.all_gather(
                triple, "tensor", axis=1, axis_index_groups=groups, tiled=True
            )
        pair_rows.append(triple)

    places = [(part, at) for part in range(parts) for at in range(part_pairs)]
    ticket = jnp.zeros((1,), jnp.int32)
    kept = ()
    for number, (part, at) in enumerate(places):
        piece = (tree.tensor, part_pairs, local_pairs, at, part * part_pairs + at)
        waits = []
        if number in (0, 1, 3):
            feed_chain.held = hold(feed_chain.held, *(kept or triples))
            waits = held_by(feed_chain)
            feed_chain.step()
        kept = attend_forward(
            piece, ticket, triples[part], pair_rows[part], kept, waits, padded, segment_rows
        )
    mixed, logsum = kept
    mixed_rows = mixed.reshape(rows, width)
    branch_one = dot(mixed_rows, merge_full, 1, 1) + merge_shift
    middle = inputs + scale_one * branch_one
    normal_two, inverse_two = norm_parts(middle)
    normed_two = (normal_two * gain_two + shift_two).astype(BF16)
    expand_full, reduce_full = feed_chain.finish(
        tables, [expand_weight.shape[1], reduce_weight.shape[1]]
    )

    upstream = pad(cotangent).astype(F32)
    back_two = (upstream * scale_two).astype(BF16)
    feed_out, normed_two_grad, expand_grad, reduce_grad, expand_bias_grad = feed_forward(
        normed_two, back_two, expand_full, reduce_full, expand_shift
    )
    feed_chain = tree.scatter([expand_grad, reduce_grad], tables)
    normed_two_grad = normed_two_grad.astype(F32)
    branch_two = feed_out.astype(F32) + reduce_shift
    result = unpad((middle + scale_two * branch_two).astype(BF16))
    middle_grad = upstream + norm_backward(normed_two_grad, gain_two, normal_two, inverse_two)
    back_one = (middle_grad * scale_one).astype(BF16)
    feed_chain.step()
    mixed_grad = dot(back_one, merge_full, 1, 0).astype(BF16).reshape(images, padded, width)
    merge_grad = dot(back_one, mixed_rows, 0, 0).astype(BF16)
    chains, part_grads, kept = [feed_chain], [], ()
    early, normed_one_grad = [], None
    for number, (part, at) in enumerate(places):
        piece = (tree.tensor, part_pairs, local_pairs, at, part * part_pairs + at)
        kept = attend_backward(
            piece,
            ticket,
            triples[part],
            pair_rows[part],
            mixed,
            mixed_grad,
            logsum,
            kept,
            held_by(*chains) + early,
            padded,
            segment_rows,
        )
        waiting = [chain for chain in chains if not chain.issued()]
        held = hold([array for chain in waiting for array in chain.held], *kept)
        for chain in waiting:
            chain.held = [held.pop(0) for _ in chain.held]
            chain.step()
        if at == part_pairs - 1:
            grad = join_grads(kept, tree.tensor * part_pairs, shares, tree.tensor)
            grad = grad.reshape(rows, -1)
            part_grads.append(grad)
            kept = ()
            sent = [dot(normed_one, grad, 0, 0).astype(BF16)]
            if part == 0:
                sent.append(merge_grad)
            chains.append(tree.scatter(sent, tables))
            term = dot(grad, triple_full[part], 1, 1)
            normed_one_grad = term if normed_one_grad is None else normed_one_grad + term
            early = [normed_one_grad]
    for chain in chains:
        chain.step()
    late_gain = after(gain_one, *held_by(chains[-1]))
    chains[-1].step()
    tokens_grad = middle_grad + norm_backward(normed_one_grad, late_gain, normal_one, inverse_one)
    tokens_grad = unpad(tokens_grad.astype(BF16))
    expand_out, reduce_out = chains[0].finish()
    first_out, merge_out = chains[1].finish()
    triple_parts = [first_out] + [chain.finish()[0] for chain in chains[2:]]
    triple_out = jnp.concatenate(
        [part.reshape(shard_rows, part_pairs, 3, PAIR) for part in triple_parts], axis=1
    )
    triple_out = triple_out.transpose(0, 2, 1, 3).reshape(shard_rows, 3, local)

    bias_sums = jnp.stack(
        [
            jnp.sum(grad, axis=0, dtype=F32).reshape(tree.tensor, part_pairs, 3, PAIR)
            for grad in part_grads
        ],
        axis=1,
    )
    sums = [
        jnp.sum(normed_one_grad * normal_one, axis=0),
        jnp.sum(normed_one_grad, axis=0),
        bias_sums[:, :, :, 0].reshape(-1),
        bias_sums[:, :, :, 2].reshape(-1),
        jnp.sum(middle_grad, axis=0) * scale_one,
        jnp.sum(middle_grad * branch_one, axis=0),
        jnp.sum(normed_two_grad * normal_two, axis=0),
        jnp.sum(normed_two_grad, axis=0),
        jnp.sum(upstream, axis=0) * scale_two,
        jnp.sum(upstream * branch_two, axis=0),
        expand_bias_grad,
    ]
    columns = jnp.concatenate(
        [total.reshape(tree.dp, -1, short) for total in sums[:-1]]
        + [sums[-1].reshape(tree.dp, -1, short)],
        axis=1,
    )
    mine = tree.scatter_rows(jnp.pad(columns, ((0, 0),) + spare))
    vector_out = [mine[place, :short] for place in range(len(vectors))]
    vector_out.append(mine[len(vectors) : packed.shape[0], :short].reshape(-1))
    return (
        result,
        tokens_grad,
        vector_out[0],
        vector_out[1],
        triple_out,
        vector_out[2],
        vector_out[3],
        merge_out,
        vector_out[4],
        vector_out[5],
        vector_out[6],
        vector_out[7],
        expand_out,
        vector_out[10],
        reduce_out,
        vector_out[8],
        vector_out[9],
    )


def solution(mesh):
    rows = P(("dp", "tensor"), None)
    vector = P("dp")
    weight = P("dp", "tensor")
    triple = P("dp", None, "tensor")
    parameters = (
        vector,
        vector,
        triple,
        vector,
        vector,
        weight,
        vector,
        vector,
        vector,
        vector,
        weight,
        vector,
        weight,
        vector,
        vector,
    )
    return jax.shard_map(
        functools.partial(body, mesh),
        mesh=mesh,
        in_specs=(rows, rows) + parameters,
        out_specs=(rows, rows) + parameters,
        check_vma=False,
    )
```

```python
import functools

import jax
import jax.numpy as jnp
from jax import lax
from jax.experimental import pallas as pl
from jax.experimental.pallas import tpu as pltpu
from jax.sharding import PartitionSpec as P

HD = 64
SEQ = 1370
PAIR = 128
F32 = jnp.float32
BF16 = jnp.bfloat16
FACTOR = HD ** (-0.5)
FACTOR_2 = FACTOR * 1.4426950408889634
VMEM = 56 * 2**20


def dot(left, right, left_dim, right_dim):
    dims = (((left_dim,), (right_dim,)), ((), ()))
    return lax.dot_general(left, right, dims, preferred_element_type=F32)


class Tree:
    def __init__(self, mesh):
        self.dp = mesh.shape["dp"]
        self.tensor = mesh.shape["tensor"]
        dp_bits = self.dp.bit_length() - 1
        tensor_bits = self.tensor.bit_length() - 1
        if 1 << dp_bits != self.dp or 1 << tensor_bits != self.tensor or dp_bits < 2:
            raise ValueError("mesh sizes")
        high = [("dp", tuple(range(dp_bits - 1, 1, -1)))]
        tensor_stages = [("tensor", (bit,)) for bit in range(tensor_bits - 1, -1, -1)]
        self.orders = (
            high + [("dp", (1,))] + tensor_stages,
            high + tensor_stages + [("dp", (1,))],
        )
        self.half_blocks = self.dp * self.tensor // 2

    def masks(self, stage):
        bits = stage[1]
        return [
            sum(1 << bit for place, bit in enumerate(bits) if choice >> place & 1)
            for choice in range(1, 1 << len(bits))
        ]

    def swap(self, value, axis, mask):
        size = self.dp if axis == "dp" else self.tensor
        return lax.ppermute(value, axis, [(i, i ^ mask) for i in range(size)])

    def spread(self, held, stage):
        return jnp.concatenate(
            [held] + [self.swap(held, stage[0], mask) for mask in self.masks(stage)], axis=0
        )

    def add_up(self, held, stage):
        size = held.shape[0] >> len(stage[1])
        total = held[:size]
        for place, mask in enumerate(self.masks(stage), 1):
            total = total + self.swap(held[place * size : (place + 1) * size], stage[0], mask)
        return total

    def tables(self):
        me_dp = lax.axis_index("dp")
        me_tensor = lax.axis_index("tensor")
        place = jnp.arange(self.half_blocks, dtype=jnp.int32)
        pairs = self.dp // 2
        relative = {
            "dp": ((place % pairs) << 1) ^ (me_dp & ~1),
            "tensor": (place // pairs) ^ me_tensor,
        }
        rows = []
        for order in self.orders:
            index = jnp.zeros_like(place)
            flat = [(axis, bit) for axis, bits in order for bit in bits]
            for position, (axis, bit) in enumerate(flat):
                index = index + (((relative[axis] >> bit) & 1) << position)
            rows.append(index)
        core = jnp.full_like(place, me_dp & 1)
        return jnp.stack(rows + [core]).astype(jnp.int32)

    def gather(self, shard):
        return Gather(self, [shard[None]])

    def assemble(self, pieces, tables, half, widths):
        pairs = self.dp // 2
        total = sum(widths)
        if 4 * half * self.half_blocks * total < 5 * 2**20:
            return self.assemble_whole(pieces, tables, half, widths)

        def kernel(tables_ref, own_a, far_a, own_b, far_b, *outs):
            core = tables_ref[2, 0]

            def put(first_a, second_a, first_b, second_b):
                at = 0
                for out, width in zip(outs, widths):
                    columns = slice(at, at + width)
                    out[0:half] = first_a[:, columns]
                    out[half : 2 * half] = first_b[:, columns]
                    out[2 * half : 3 * half] = second_a[:, columns]
                    out[3 * half : 4 * half] = second_b[:, columns]
                    at += width

            @pl.when(core == 0)
            def _():
                put(own_a, far_a, own_b, far_b)

            @pl.when(core != 0)
            def _():
                put(far_a, own_a, far_b, own_b)

        spec_a = pl.BlockSpec((None, half, total), lambda i, table: (table[0, i], 0, 0))
        spec_b = pl.BlockSpec((None, half, total), lambda i, table: (table[1, i], 0, 0))
        return pl.pallas_call(
            kernel,
            grid_spec=pltpu.PrefetchScalarGridSpec(
                num_scalar_prefetch=1,
                grid=(self.half_blocks,),
                in_specs=[spec_a, spec_a, spec_b, spec_b],
                out_specs=[
                    pl.BlockSpec((4 * half, width), lambda i, table: (i % pairs, i // pairs))
                    for width in widths
                ],
            ),
            out_shape=[
                jax.ShapeDtypeStruct((self.dp * 2 * half, self.tensor * width), BF16)
                for width in widths
            ],
            compiler_params=pltpu.CompilerParams(vmem_limit_bytes=VMEM),
        )(tables, *pieces)

    def assemble_whole(self, pieces, tables, half, widths):
        pairs = self.dp // 2

        def kernel(tables_ref, own_a, far_a, own_b, far_b, *outs):
            core = tables_ref[2, 0]

            @pl.loop(0, pairs)
            def _(pair):
                own = pl.multiple_of((2 * pair + core) * 2 * half, 2 * half)
                far = pl.multiple_of((2 * pair + 1 - core) * 2 * half, 2 * half)
                for tensor in range(self.tensor):
                    at_a = tables_ref[0, tensor * pairs + pair]
                    at_b = tables_ref[1, tensor * pairs + pair]
                    at = 0
                    for out, width in zip(outs, widths):
                        source = slice(at, at + width)
                        columns = slice(tensor * width, (tensor + 1) * width)
                        out[pl.ds(own, half), columns] = own_a[at_a, :, source]
                        out[pl.ds(own + half, half), columns] = own_b[at_b, :, source]
                        out[pl.ds(far, half), columns] = far_a[at_a, :, source]
                        out[pl.ds(far + half, half), columns] = far_b[at_b, :, source]
                        at += width

        return self.whole_call(
            kernel,
            tables,
            pieces,
            [(self.dp * 2 * half, self.tensor * width) for width in widths],
        )

    def split_whole(self, arrays, tables, half, widths):
        pairs = self.dp // 2

        def kernel(tables_ref, *refs):
            sources, (own_a, far_a, own_b, far_b) = refs[: len(widths)], refs[len(widths) :]
            core = tables_ref[2, 0]

            @pl.loop(0, pairs)
            def _(pair):
                own = pl.multiple_of((2 * pair + core) * 2 * half, 2 * half)
                far = pl.multiple_of((2 * pair + 1 - core) * 2 * half, 2 * half)
                for tensor in range(self.tensor):
                    at_a = tables_ref[0, tensor * pairs + pair]
                    at_b = tables_ref[1, tensor * pairs + pair]
                    at = 0
                    for source, width in zip(sources, widths):
                        target = slice(at, at + width)
                        columns = slice(tensor * width, (tensor + 1) * width)
                        own_a[at_a, :, target] = source[pl.ds(own, half), columns]
                        own_b[at_b, :, target] = source[pl.ds(own + half, half), columns]
                        far_a[at_a, :, target] = source[pl.ds(far, half), columns]
                        far_b[at_b, :, target] = source[pl.ds(far + half, half), columns]
                        at += width

        return self.whole_call(
            kernel, tables, arrays, [(self.half_blocks, half, sum(widths))] * 4
        )

    def whole_call(self, kernel, tables, values, shapes):
        vmem = pl.BlockSpec(memory_space=pltpu.VMEM)
        return pl.pallas_call(
            kernel,
            in_specs=[pl.BlockSpec(memory_space=pltpu.SMEM)] + [vmem] * len(values),
            out_specs=[vmem] * len(shapes),
            out_shape=[jax.ShapeDtypeStruct(shape, BF16) for shape in shapes],
            compiler_params=pltpu.CompilerParams(vmem_limit_bytes=VMEM),
        )(tables, *values)

    def split(self, arrays, tables, half, widths):
        pairs = self.dp // 2
        total = sum(widths)
        if 4 * half * self.half_blocks * total < 5 * 2**20:
            return self.split_whole(arrays, tables, half, widths)

        def kernel(tables_ref, *refs):
            sources, (own_a, far_a, own_b, far_b) = refs[: len(widths)], refs[len(widths) :]
            core = tables_ref[2, 0]

            def take(first_a, second_a, first_b, second_b):
                at = 0
                for source, width in zip(sources, widths):
                    columns = slice(at, at + width)
                    first_a[:, columns] = source[0:half]
                    first_b[:, columns] = source[half : 2 * half]
                    second_a[:, columns] = source[2 * half : 3 * half]
                    second_b[:, columns] = source[3 * half : 4 * half]
                    at += width

            @pl.when(core == 0)
            def _():
                take(own_a, far_a, own_b, far_b)

            @pl.when(core != 0)
            def _():
                take(far_a, own_a, far_b, own_b)

        spec_a = pl.BlockSpec((None, half, total), lambda i, table: (table[0, i], 0, 0))
        spec_b = pl.BlockSpec((None, half, total), lambda i, table: (table[1, i], 0, 0))
        shape = jax.ShapeDtypeStruct((self.half_blocks, half, total), BF16)
        return pl.pallas_call(
            kernel,
            grid_spec=pltpu.PrefetchScalarGridSpec(
                num_scalar_prefetch=1,
                grid=(self.half_blocks,),
                in_specs=[
                    pl.BlockSpec((4 * half, width), lambda i, table: (i % pairs, i // pairs))
                    for width in widths
                ],
                out_specs=[spec_a, spec_a, spec_b, spec_b],
            ),
            out_shape=[shape] * 4,
            compiler_params=pltpu.CompilerParams(vmem_limit_bytes=VMEM),
        )(tables, *arrays)

    def scatter(self, arrays, tables):
        rows = arrays[0].shape[0] // self.dp
        widths = [array.shape[1] // self.tensor for array in arrays]
        return Scatter(self, self.split(arrays, tables, rows // 2, widths), widths)

    def row_stages(self):
        bits = tuple(range(self.dp.bit_length() - 1))
        return [("dp", bits[2:]), ("dp", bits[:2])]

    def gather_rows(self, row):
        held = row[None]
        stages = self.row_stages()
        for stage in stages:
            held = self.spread(held, stage)
        relative = jnp.arange(self.dp) ^ lax.axis_index("dp")
        index = jnp.zeros_like(relative)
        for position, bit in enumerate(bit for stage in stages for bit in stage[1]):
            index = index + (((relative >> bit) & 1) << position)
        return held[index]

    def scatter_rows(self, rows):
        stages = self.row_stages()
        place = jnp.arange(self.dp)
        relative = jnp.zeros_like(place)
        for position, bit in enumerate(bit for stage in stages for bit in stage[1]):
            relative = relative + (((place >> position) & 1) << bit)
        held = rows[relative ^ lax.axis_index("dp")]
        for bit in range(self.tensor.bit_length() - 1):
            held = held + self.swap(held, "tensor", 1 << bit)
        for stage in stages[::-1]:
            held = self.add_up(held, stage)
        return held[0]


class Gather:
    def __init__(self, tree, held):
        self.tree = tree
        self.held = held
        self.done = 0
        self.stages = len(tree.orders[0])

    def step(self):
        if self.done == 0:
            whole = self.tree.spread(self.held[0], self.tree.orders[0][0])
            half = whole.shape[1] // 2
            self.held = [whole[:, :half], whole[:, half:]]
        elif self.done < self.stages:
            self.held = [
                self.tree.spread(held, order[self.done])
                for held, order in zip(self.held, self.tree.orders)
            ]
        elif self.done == self.stages:
            self.held = self.held + [self.tree.swap(held, "dp", 1) for held in self.held]
        self.done += 1

    def finish(self, tables, widths):
        while self.done <= self.stages:
            self.step()
        own_a, own_b, far_a, far_b = self.held
        half = own_a.shape[1]
        return self.tree.assemble([own_a, far_a, own_b, far_b], tables, half, widths)


class Scatter:
    def __init__(self, tree, pieces, widths):
        own_a, far_a, own_b, far_b = pieces
        self.tree = tree
        self.widths = widths
        self.held = [own_a, own_b]
        self.sent = [[far_a], [far_b]]
        self.orders = [[("dp", (0,))] + order[::-1] for order in tree.orders]
        self.done = 0

    def step(self):
        if self.issued():
            return
        totals = []
        for held, sent, order in zip(self.held, self.sent, self.orders):
            axis = order[self.done][0]
            total = held.astype(F32)
            for value, mask in zip(sent, self.tree.masks(order[self.done])):
                total = total + self.tree.swap(value, axis, mask).astype(F32)
            totals.append(total)
        self.done += 1
        if self.issued():
            self.held, self.sent = totals, []
            return
        if self.done + 1 == len(self.orders[0]):
            totals = [jnp.concatenate(totals, axis=1)]
        self.held, self.sent = [], []
        for total, order in zip(totals, self.orders):
            total = total.astype(BF16)
            count = 1 << len(order[self.done][1])
            size = total.shape[0] // count
            parts = [total[place * size : (place + 1) * size] for place in range(count)]
            self.held.append(parts[0])
            self.sent.append(parts[1:])

    def issued(self):
        return self.done == len(self.orders[0])

    def finish(self):
        while not self.issued():
            self.step()
        whole = self.held[0][0]
        parts, at = [], 0
        for width in self.widths:
            parts.append(whole[:, at : at + width])
            at += width
        return parts


def held_by(*chains):
    arrays = []
    for chain in chains:
        arrays += chain.held
        for sent in getattr(chain, "sent", ()):
            arrays += sent
    return arrays


def hold(arrays, *others):
    count = len(arrays)

    def kernel(*refs):
        refs[-1][...] = jnp.zeros(refs[-1].shape, F32)

    unread = pl.BlockSpec(memory_space=pl.ANY)
    outs = pl.pallas_call(
        kernel,
        in_specs=[unread] * (count + len(others)),
        out_specs=[unread] * count + [pl.BlockSpec(memory_space=pltpu.VMEM)],
        out_shape=[jax.ShapeDtypeStruct(array.shape, array.dtype) for array in arrays]
        + [jax.ShapeDtypeStruct((8, 128), F32)],
        input_output_aliases={place: place for place in range(count)},
    )(*arrays, *others)
    return list(outs[:count])


def after(value, *arrays):
    for array in arrays:
        value = value + (array[(0,) * array.ndim].astype(F32) * 0.0).astype(value.dtype)
    return value


def split_pair(block):
    lane = lax.broadcasted_iota(jnp.int32, block.shape, 1)
    zero = jnp.zeros_like(block)
    return jnp.concatenate(
        [jnp.where(lane < HD, block, zero), jnp.where(lane >= HD, block, zero)], axis=0
    )


def join_pair(block):
    rows = block.shape[0] // 2
    lane = lax.broadcasted_iota(jnp.int32, (rows, PAIR), 1)
    return jnp.where(lane < HD, block[:rows], block[rows:])


def mask_keys(scores, segment, valid, fill):
    if valid == segment:
        return scores
    start = valid // 128 * 128
    parts = []
    for base in range(0, scores.shape[1], segment):
        if start:
            parts.append(scores[:, base : base + start])
        tail = scores[:, base + start : base + segment]
        lane = lax.broadcasted_iota(jnp.int32, tail.shape, 1) + start
        parts.append(jnp.where(lane < valid, tail, fill))
    return jnp.concatenate(parts, axis=1)


def attend_forward_kernel(segment, valid, ticket_ref, query_ref, pair_ref, *rest):
    mixed_ref, logsum_ref, value_ref = rest[-3:]
    keys = pair_ref.at[:, PAIR : 2 * PAIR]
    value_ref[:, 0:PAIR] = pair_ref[:, 2 * PAIR : 3 * PAIR]
    value_ref[:, PAIR : 2 * PAIR] = jnp.ones((value_ref.shape[0], PAIR), BF16)
    for chunk in range(query_ref.shape[0] // 128):
        rows = pl.ds(chunk * 128, 128)
        queries = split_pair(query_ref[rows, 0:PAIR])
        scores = mask_keys(dot(queries, keys[...], 1, 1), segment, valid, -1e30)
        peak = jnp.max(scores, axis=1, keepdims=True)
        weights = jnp.exp2((scores - peak) * FACTOR_2).astype(BF16)
        mixed = dot(weights, value_ref[...], 1, 0)
        total = mixed[:, PAIR:]
        mixed_ref[rows, :] = join_pair(mixed[:, :PAIR] / total).astype(BF16)
        logsum_ref[rows, :] = join_pair(peak * FACTOR_2 + jnp.log2(total))


def attend_backward_kernel(
    segment, valid, joint, ticket_ref, query_ref, pair_ref, mixed_ref, grad_ref, logsum_ref, *rest
):
    if joint:
        out_ref, key_sum, value_sum = rest[-3:]
        query_out = out_ref.at[:, 0:PAIR]
        key_out = out_ref.at[:, PAIR : 2 * PAIR]
        value_out = out_ref.at[:, 2 * PAIR : 3 * PAIR]
    else:
        query_out, pair_out, key_sum, value_sum = rest[-4:]
        key_out = pair_out.at[:, 0:PAIR]
        value_out = pair_out.at[:, PAIR : 2 * PAIR]
    keys = pair_ref.at[:, PAIR : 2 * PAIR]
    values = pair_ref.at[:, 2 * PAIR : 3 * PAIR]
    key_total = value_total = None
    for chunk in range(query_ref.shape[0] // 128):
        rows = pl.ds(chunk * 128, 128)
        queries = split_pair(query_ref[rows, 0:PAIR])
        grad = grad_ref[rows, :]
        grads = split_pair(grad)
        row_term = jnp.sum(
            split_pair(grad.astype(F32) * mixed_ref[rows, :].astype(F32)), axis=1, keepdims=True
        )
        logsum = logsum_ref[rows, :]
        logsum = jnp.concatenate([logsum[:, 0:1], logsum[:, HD : HD + 1]], axis=0)
        scores = dot(queries, keys[...], 1, 1)
        probs = mask_keys(jnp.exp2(scores * FACTOR_2 - logsum), segment, valid, 0.0)
        prob_grad = dot(grads, values[...], 1, 1)
        score_grad = (probs * (prob_grad - row_term)).astype(BF16)
        query_grad = join_pair(dot(score_grad, keys[...], 1, 0)) * FACTOR
        query_out[rows, :] = query_grad.astype(BF16)
        value_part = dot(grads.T, probs.astype(BF16), 1, 0)
        key_part = dot(queries.T, score_grad, 1, 0)
        if chunk == 0:
            value_sum[...] = value_part
            key_sum[...] = key_part
        else:
            value_sum[...] += value_part
            key_sum[...] += key_part
    key_out[...] = (key_sum[...] * FACTOR).T.astype(BF16)
    value_out[...] = value_sum[...].T.astype(BF16)


def attend_cost(products, images, pairs, rows, key_rows):
    area = images * pairs * 2 * rows * key_rows
    return pl.CostEstimate(
        flops=2 * products * area * HD * 4,
        bytes_accessed=images * pairs * rows * PAIR * 16,
        transcendentals=area,
    )


def attend_forward(piece, ticket, triple, gathered, kept, waits, segment, valid):
    groups, part_pairs, all_pairs, part_at, all_at = piece
    images, rows, _ = triple.shape
    key_rows = gathered.shape[1]
    pairs = groups * all_pairs
    narrow = lambda i, g, t: (i, 0, g * part_pairs + part_at)
    wide = lambda i, g, t: (i, 0, g * all_pairs + all_at)
    unread = pl.BlockSpec(memory_space=pl.ANY)
    return pl.pallas_call(
        functools.partial(attend_forward_kernel, segment, valid),
        grid_spec=pltpu.PrefetchScalarGridSpec(
            num_scalar_prefetch=1,
            grid=(images, groups),
            in_specs=[
                pl.BlockSpec((None, rows, 3 * PAIR), narrow),
                pl.BlockSpec((None, key_rows, 3 * PAIR), narrow),
            ]
            + [unread] * (len(kept) + len(waits)),
            out_specs=[
                pl.BlockSpec((None, rows, PAIR), wide),
                pl.BlockSpec((None, rows, PAIR), wide),
            ],
            scratch_shapes=[pltpu.VMEM((key_rows, 2 * PAIR), BF16)],
        ),
        out_shape=[
            jax.ShapeDtypeStruct((images, rows, pairs * PAIR), BF16),
            jax.ShapeDtypeStruct((images, rows, pairs * PAIR), F32),
        ],
        input_output_aliases={3 + place: place for place in range(len(kept))},
        cost_estimate=attend_cost(2, images, groups, rows, key_rows),
        compiler_params=pltpu.CompilerParams(vmem_limit_bytes=VMEM),
    )(ticket, triple, gathered, *kept, *waits)


def attend_backward(
    piece, ticket, triple, gathered, mixed, mixed_grad, logsum, kept, waits, segment, valid
):
    groups, part_pairs, all_pairs, part_at, all_at = piece
    images, rows, width = triple.shape
    key_rows = gathered.shape[1]
    joint = key_rows == rows
    narrow = lambda i, g, t: (i, 0, g * part_pairs + part_at)
    wide = lambda i, g, t: (i, 0, g * all_pairs + all_at)
    wide_spec = pl.BlockSpec((None, rows, PAIR), wide)
    triple_spec = pl.BlockSpec((None, rows, 3 * PAIR), narrow)
    pairs = groups * part_pairs
    if joint:
        out_specs = [triple_spec]
        out_shape = [jax.ShapeDtypeStruct(triple.shape, BF16)]
    else:
        out_specs = [
            pl.BlockSpec((None, rows, PAIR), narrow),
            pl.BlockSpec((None, key_rows, 2 * PAIR), narrow),
        ]
        out_shape = [
            jax.ShapeDtypeStruct((images, rows, pairs * PAIR), BF16),
            jax.ShapeDtypeStruct((images, key_rows, pairs * 2 * PAIR), BF16),
        ]
    return pl.pallas_call(
        functools.partial(attend_backward_kernel, segment, valid, joint),
        grid_spec=pltpu.PrefetchScalarGridSpec(
            num_scalar_prefetch=1,
            grid=(images, groups),
            in_specs=[
                triple_spec,
                pl.BlockSpec((None, key_rows, 3 * PAIR), narrow),
                wide_spec,
                wide_spec,
                wide_spec,
            ]
            + [pl.BlockSpec(memory_space=pl.ANY)] * (len(kept) + len(waits)),
            out_specs=out_specs,
            scratch_shapes=[pltpu.VMEM((PAIR, key_rows), F32)] * 2,
        ),
        out_shape=out_shape,
        input_output_aliases={6 + place: place for place in range(len(kept))},
        cost_estimate=attend_cost(5, images, groups, rows, key_rows),
        compiler_params=pltpu.CompilerParams(vmem_limit_bytes=VMEM),
    )(ticket, triple, gathered, mixed, mixed_grad, logsum, *kept, *waits)


def join_grads(outs, pairs, shares, tensor):
    if len(outs) == 1:
        return outs[0]
    query_grad, pair_grad = outs
    images, rows, _ = query_grad.shape
    groups = [list(range(base, base + shares)) for base in range(0, tensor, shares)]
    pair_grad = lax.psum_scatter(
        pair_grad, "tensor", scatter_dimension=1, axis_index_groups=groups, tiled=True
    )
    return jnp.concatenate(
        [
            query_grad.reshape(images, rows, pairs, PAIR),
            pair_grad.reshape(images, rows, pairs, 2 * PAIR),
        ],
        axis=3,
    ).reshape(images, rows, pairs * 3 * PAIR)


def norm_parts(values):
    centre = jnp.mean(values, axis=-1, keepdims=True)
    centred = values - centre
    spread = jnp.mean(centred * centred, axis=-1, keepdims=True)
    inverse = lax.rsqrt(spread + 1e-06)
    return centred * inverse, inverse


def norm_backward(grad, gain, normed, inverse):
    scaled = grad * gain
    return inverse * (
        scaled
        - jnp.mean(scaled, axis=-1, keepdims=True)
        - normed * jnp.mean(scaled * normed, axis=-1, keepdims=True)
    )


TAIL_RATE = 0.3275911 * 0.5**0.5
TAIL = (0.5307027145, -0.7265760135, 0.7107068705, -0.142248368, 0.127414796)


def gelu_parts(values):
    point = 1.0 / (1.0 + TAIL_RATE * jnp.abs(values))
    total = TAIL[0] * point
    for factor in TAIL[1:]:
        total = (total + factor) * point
    bell = jnp.exp2((-0.5 * 1.4426950408889634) * (values * values))
    tail = total * bell
    below = jnp.where(values < 0.0, tail, 1.0 - tail)
    return values * below, below + (values * 0.3989422804014327) * bell


def feed_kernel(tile, *refs):
    (normed_ref, back_ref, expand_ref, reduce_ref, bias_ref) = refs[:5]
    (out_ref, grad_ref, expand_out, reduce_out, bias_out) = refs[5:10]
    (out_sum, grad_sum, active_ref, gate_ref, stage_ref) = refs[10:]
    rows = normed_ref.shape[0]
    expand = expand_ref[...]
    reduce = reduce_ref[...]
    bias = bias_ref[0:1, :]

    def tiles(first):
        total = None
        here = pl.ds(0, tile)
        ahead = (dot(normed_ref[here, :], expand, 1, 0), dot(back_ref[here, :], reduce, 1, 0))
        for base in range(0, rows, tile):
            here = pl.ds(base, tile)
            forward, backward = ahead
            if base + tile < rows:
                coming = pl.ds(base + tile, tile)
                ahead = (
                    dot(normed_ref[coming, :], expand, 1, 0),
                    dot(back_ref[coming, :], reduce, 1, 0),
                )
            active, slope = gelu_parts(forward + bias)
            active = active.astype(BF16)
            gate = backward * slope
            part = jnp.sum(gate.reshape(tile // 8, 8, gate.shape[1]), axis=0)
            total = part if total is None else total + part
            gate = gate.astype(BF16)
            active_ref[here, :] = active
            gate_ref[here, :] = gate
            out = dot(active, reduce, 1, 1)
            grad = dot(gate, expand, 1, 1)
            if first:
                out_sum[here, :] = out
                grad_sum[here, :] = grad
            else:
                out_sum[here, :] += out
                grad_sum[here, :] += grad
        bias_out[...] = total

    @pl.when(pl.program_id(0) == 0)
    def _():
        tiles(True)

    @pl.when(pl.program_id(0) != 0)
    def _():
        tiles(False)

    reduce_out[...] = dot(active_ref[...], back_ref[...], 0, 0).T.astype(BF16)
    expand_out[...] = dot(gate_ref[...], normed_ref[...], 0, 0).T.astype(BF16)

    @pl.when(pl.program_id(0) == pl.num_programs(0) - 1)
    def _():
        stage_rows = stage_ref.shape[0]

        @pl.loop(0, rows // stage_rows)
        def _(i):
            here = pl.ds(pl.multiple_of(i * stage_rows, stage_rows), stage_rows)
            stage_ref[...] = out_sum[here, :].astype(BF16)
            pltpu.sync_copy(stage_ref, out_ref.at[here, :])
            stage_ref[...] = grad_sum[here, :].astype(BF16)
            pltpu.sync_copy(stage_ref, grad_ref.at[here, :])


def feed_forward(normed, back, expand, reduce, bias):
    rows, width = normed.shape
    hidden = expand.shape[1]
    block = 256
    tile = rows // 4
    whole = pl.BlockSpec(memory_space=pltpu.VMEM)
    left = pl.BlockSpec(memory_space=pl.ANY)
    columns = pl.BlockSpec((width, block), lambda f: (0, f))
    vector = pl.BlockSpec((8, block), lambda f: (0, f))
    bias = jnp.broadcast_to(bias[None], (8, hidden))
    out, grad, expand_grad, reduce_grad, bias_grad = pl.pallas_call(
        functools.partial(feed_kernel, tile),
        grid=(hidden // block,),
        in_specs=[whole, whole, columns, columns, vector],
        out_specs=[left, left, columns, columns, vector],
        out_shape=[
            jax.ShapeDtypeStruct((rows, width), BF16),
            jax.ShapeDtypeStruct((rows, width), BF16),
            jax.ShapeDtypeStruct((width, hidden), BF16),
            jax.ShapeDtypeStruct((width, hidden), BF16),
            jax.ShapeDtypeStruct((8, hidden), F32),
        ],
        scratch_shapes=[
            pltpu.VMEM((rows, width), F32),
            pltpu.VMEM((rows, width), F32),
            pltpu.VMEM((rows, block), BF16),
            pltpu.VMEM((rows, block), BF16),
            pltpu.VMEM((128, width), BF16),
        ],
        cost_estimate=pl.CostEstimate(
            flops=12 * rows * width * hidden,
            bytes_accessed=8 * rows * width + 8 * width * hidden,
            transcendentals=rows * hidden,
        ),
        compiler_params=pltpu.CompilerParams(vmem_limit_bytes=60 * 2**20),
    )(normed, back, expand, reduce, bias)
    return out, grad, expand_grad, reduce_grad, jnp.sum(bias_grad, axis=0)


def body(
    mesh,
    tokens,
    cotangent,
    attention_gain,
    attention_shift,
    triple_weight,
    query_bias,
    value_bias,
    merge_weight,
    merge_bias,
    attention_scale,
    forward_gain,
    forward_shift,
    expand_weight,
    expand_bias,
    reduce_weight,
    reduce_bias,
    forward_scale,
):
    tree = Tree(mesh)
    tables = tree.tables()
    count, width = tokens.shape
    segment_rows = min(count, SEQ)
    images = count // segment_rows
    shares = SEQ // segment_rows
    if images * segment_rows != count or shares * segment_rows != SEQ:
        raise ValueError("token rows")
    padded = -(-segment_rows // 128) * 128
    rows = images * padded

    def pad(values):
        shaped = values.reshape(images, segment_rows, width)
        shaped = jnp.pad(shaped, ((0, 0), (0, padded - segment_rows), (0, 0)))
        return shaped.reshape(rows, width)

    def unpad(values):
        return values.reshape(images, padded, width)[:, :segment_rows].reshape(count, width)

    vectors = [
        attention_gain,
        attention_shift,
        query_bias,
        value_bias,
        merge_bias,
        attention_scale,
        forward_gain,
        forward_shift,
        reduce_bias,
        forward_scale,
    ]
    short = attention_gain.shape[0]
    packed = jnp.concatenate([jnp.stack(vectors), expand_bias.reshape(-1, short)], axis=0)
    spare = ((0, -packed.shape[0] % 8), (0, -short % 128))
    gathered = tree.gather_rows(jnp.pad(packed.astype(F32), spare))
    (
        gain_one,
        shift_one,
        query_shift,
        value_shift,
        merge_shift,
        scale_one,
        gain_two,
        shift_two,
        reduce_shift,
        scale_two,
    ) = [gathered[:, place, :short].reshape(-1) for place in range(len(vectors))]
    expand_shift = gathered[:, len(vectors) : packed.shape[0], :short].reshape(-1)

    shard_rows, _, local = triple_weight.shape
    local_pairs = local // PAIR
    parts = 2 if local_pairs % 2 == 0 else 1
    part_pairs = local_pairs // parts
    part_width = part_pairs * 3 * PAIR
    triple_shard = (
        triple_weight.reshape(shard_rows, 3, local_pairs, PAIR)
        .transpose(0, 2, 1, 3)
        .reshape(shard_rows, 3 * local)
    )
    inputs = pad(tokens).astype(F32)
    normal_one, inverse_one = norm_parts(inputs)
    normed_one = (normal_one * gain_one + shift_one).astype(BF16)
    first = tree.gather(jnp.concatenate([triple_shard, merge_weight], axis=1))
    first.step()
    feed_chain = tree.gather(
        after(jnp.concatenate([expand_weight, reduce_weight], axis=1), *first.held)
    )
    feed_chain.step()
    first.step()
    while first.done < first.stages:
        first.step()
    first.step()
    *triple_full, merge_full = first.finish(
        tables, [part_width] * parts + [merge_weight.shape[1]]
    )
    pairs = tree.tensor * local_pairs
    bias = jnp.stack(
        [
            query_shift.reshape(tree.tensor, parts, part_pairs, PAIR),
            jnp.zeros((tree.tensor, parts, part_pairs, PAIR), F32),
            value_shift.reshape(tree.tensor, parts, part_pairs, PAIR),
        ],
        axis=3,
    )
    triples, pair_rows = [], []
    for part in range(parts):
        triple = dot(normed_one, triple_full[part], 1, 0) + bias[:, part].reshape(-1)
        triple = triple.astype(BF16).reshape(images, padded, -1)
        triples.append(triple)
        if shares > 1:
            groups = [list(range(base, base + shares)) for base in range(0, tree.tensor, shares)]
            triple = lax.all_gather(
                triple, "tensor", axis=1, axis_index_groups=groups, tiled=True
            )
        pair_rows.append(triple)

    places = [(part, at) for part in range(parts) for at in range(part_pairs)]
    ticket = jnp.zeros((1,), jnp.int32)
    kept = ()
    for number, (part, at) in enumerate(places):
        piece = (tree.tensor, part_pairs, local_pairs, at, part * part_pairs + at)
        waits = []
        if number in (0, 1, 3):
            feed_chain.held = hold(feed_chain.held, *(kept or triples))
            waits = held_by(feed_chain)
            feed_chain.step()
        kept = attend_forward(
            piece, ticket, triples[part], pair_rows[part], kept, waits, padded, segment_rows
        )
    mixed, logsum = kept
    mixed_rows = mixed.reshape(rows, width)
    branch_one = dot(mixed_rows, merge_full, 1, 1) + merge_shift
    middle = inputs + scale_one * branch_one
    normal_two, inverse_two = norm_parts(middle)
    normed_two = (normal_two * gain_two + shift_two).astype(BF16)
    expand_full, reduce_full = feed_chain.finish(
        tables, [expand_weight.shape[1], reduce_weight.shape[1]]
    )

    upstream = pad(cotangent).astype(F32)
    back_two = (upstream * scale_two).astype(BF16)
    feed_out, normed_two_grad, expand_grad, reduce_grad, expand_bias_grad = feed_forward(
        normed_two, back_two, expand_full, reduce_full, expand_shift
    )
    feed_chain = tree.scatter([expand_grad, reduce_grad], tables)
    normed_two_grad = normed_two_grad.astype(F32)
    branch_two = feed_out.astype(F32) + reduce_shift
    result = unpad((middle + scale_two * branch_two).astype(BF16))
    middle_grad = upstream + norm_backward(normed_two_grad, gain_two, normal_two, inverse_two)
    back_one = (middle_grad * scale_one).astype(BF16)
    feed_chain.step()
    mixed_grad = dot(back_one, merge_full, 1, 0).astype(BF16).reshape(images, padded, width)
    merge_grad = dot(back_one, mixed_rows, 0, 0).astype(BF16)
    chains, part_grads, kept = [feed_chain], [], ()
    early, normed_one_grad = [], None
    for number, (part, at) in enumerate(places):
        piece = (tree.tensor, part_pairs, local_pairs, at, part * part_pairs + at)
        kept = attend_backward(
            piece,
            ticket,
            triples[part],
            pair_rows[part],
            mixed,
            mixed_grad,
            logsum,
            kept,
            held_by(*chains) + early,
            padded,
            segment_rows,
        )
        waiting = [chain for chain in chains if not chain.issued()]
        held = hold([array for chain in waiting for array in chain.held], *kept)
        for chain in waiting:
            chain.held = [held.pop(0) for _ in chain.held]
            chain.step()
        if at == part_pairs - 1:
            grad = join_grads(kept, tree.tensor * part_pairs, shares, tree.tensor)
            grad = grad.reshape(rows, -1)
            part_grads.append(grad)
            kept = ()
            sent = [dot(normed_one, grad, 0, 0).astype(BF16)]
            if part == 0:
                sent.append(merge_grad)
            chains.append(tree.scatter(sent, tables))
            term = dot(grad, triple_full[part], 1, 1)
            normed_one_grad = term if normed_one_grad is None else normed_one_grad + term
            early = [normed_one_grad]
    for chain in chains:
        chain.step()
    late_gain = after(gain_one, *held_by(chains[-1]))
    chains[-1].step()
    tokens_grad = middle_grad + norm_backward(normed_one_grad, late_gain, normal_one, inverse_one)
    tokens_grad = unpad(tokens_grad.astype(BF16))
    expand_out, reduce_out = chains[0].finish()
    first_out, merge_out = chains[1].finish()
    triple_parts = [first_out] + [chain.finish()[0] for chain in chains[2:]]
    triple_out = jnp.concatenate(
        [part.reshape(shard_rows, part_pairs, 3, PAIR) for part in triple_parts], axis=1
    )
    triple_out = triple_out.transpose(0, 2, 1, 3).reshape(shard_rows, 3, local)

    bias_sums = jnp.stack(
        [
            jnp.sum(grad, axis=0, dtype=F32).reshape(tree.tensor, part_pairs, 3, PAIR)
            for grad in part_grads
        ],
        axis=1,
    )
    sums = [
        jnp.sum(normed_one_grad * normal_one, axis=0),
        jnp.sum(normed_one_grad, axis=0),
        bias_sums[:, :, :, 0].reshape(-1),
        bias_sums[:, :, :, 2].reshape(-1),
        jnp.sum(middle_grad, axis=0) * scale_one,
        jnp.sum(middle_grad * branch_one, axis=0),
        jnp.sum(normed_two_grad * normal_two, axis=0),
        jnp.sum(normed_two_grad, axis=0),
        jnp.sum(upstream, axis=0) * scale_two,
        jnp.sum(upstream * branch_two, axis=0),
        expand_bias_grad,
    ]
    columns = jnp.concatenate(
        [total.reshape(tree.dp, -1, short) for total in sums[:-1]]
        + [sums[-1].reshape(tree.dp, -1, short)],
        axis=1,
    )
    mine = tree.scatter_rows(jnp.pad(columns, ((0, 0),) + spare))
    vector_out = [mine[place, :short] for place in range(len(vectors))]
    vector_out.append(mine[len(vectors) : packed.shape[0], :short].reshape(-1))
    return (
        result,
        tokens_grad,
        vector_out[0],
        vector_out[1],
        triple_out,
        vector_out[2],
        vector_out[3],
        merge_out,
        vector_out[4],
        vector_out[5],
        vector_out[6],
        vector_out[7],
        expand_out,
        vector_out[10],
        reduce_out,
        vector_out[8],
        vector_out[9],
    )


def solution(mesh):
    rows = P(("dp", "tensor"), None)
    vector = P("dp")
    weight = P("dp", "tensor")
    triple = P("dp", None, "tensor")
    parameters = (
        vector,
        vector,
        triple,
        vector,
        vector,
        weight,
        vector,
        vector,
        vector,
        vector,
        weight,
        vector,
        weight,
        vector,
        vector,
    )
    return jax.shard_map(
        functools.partial(body, mesh),
        mesh=mesh,
        in_specs=(rows, rows) + parameters,
        out_specs=(rows, rows) + parameters,
        check_vma=False,
    )
```
